32 devices in a mesh: gx: 4 (over x, core), gy: 4 (over z), gz: 2 (over y).
Axes of the slice: x: 2, y: 2, z: 4, core: 2. Of those that a mesh axis runs over, the one named last changes fastest.
Arguments:
- densities: bfloat16 [128, 32, 8, 448], P('gx', 'gy', 'gz'), may hold values from -6 to 6
- upward_weight: bfloat16 [448, 56], replicated, may hold values from -0.25 to 0.25
- transfer_weight: bfloat16 [316, 56, 56], replicated, may hold values from -0.0625 to 0.0625
- downward_weight: bfloat16 [56, 448], replicated, may hold values from -0.75 to 0.75
Outputs:
- leaf_locals: float32 [128, 32, 8, 448], P('gx', 'gy', 'gz')
The draws below stay inside these ranges and needn't reach their ends.
All inputs are finite; a program needn't handle non-finite values.
Results may differ from the reference program's by a relative error of at most 0.0045.
Values may be sent and summed in bfloat16 or wider, within the bound.
No kernel may reach another device: no remote copies, remote signals or barrier semaphores. Data moves between devices by JAX's collectives and lax.ppermute only.
A program may use at most 128 MiB of HBM per device.

```python
import jax
import jax.numpy as jnp
from jax import lax

NCOEF = 56
OFFSETS = 316
NX = 256
NY = 64
NZ = 16


def shard_levels(stream_key, shape, split, low, top_value):
    factor_of = 1.0
    for dim, blocks in split:
        heights = jax.random.uniform(jax.random.fold_in(jax.random.fold_in(stream_key, 6), dim), (blocks,), jnp.float32, low / len(split), top_value / len(split))
        factor_of = factor_of * jnp.repeat(jnp.exp(heights), shape[dim] // blocks).reshape((-1,) + (1,) * (len(shape) - 1 - dim))
    return factor_of


def bell_draw(key, dims, spread, bound, cuts=(), kind=jnp.bfloat16):
    array = jax.random.normal(key, dims, jnp.float32) * spread
    if len(cuts) > 0:
        array = shard_levels(key, dims, cuts, -0.22, 0.18) * array
    return jnp.clip(array, min=-bound, max=bound).astype(kind)


def setup_inputs(seed: int = 0) -> dict:
    key_list = jax.random.split(jax.random.key(seed), 5)
    return {
        "densities": bell_draw(key_list[0], (NX // 2, NY // 2, NZ // 2, 8 * NCOEF), 1.0, 6.0, ((0, 4), (1, 4), (2, 2))),
        "upward_weight": bell_draw(key_list[1], (8 * NCOEF, NCOEF), (8 * NCOEF) ** -0.5, 0.25),
        "transfer_weight": bell_draw(key_list[2], (OFFSETS, NCOEF, NCOEF), (189 * NCOEF) ** -0.5, 0.0625),
        "downward_weight": bell_draw(key_list[3], (NCOEF, 8 * NCOEF), NCOEF ** -0.5, 0.75),
    }


def kernel_table(transfer_weight):
    coeffs = transfer_weight.shape[1]
    empty = jnp.zeros((coeffs, coeffs), transfer_weight.dtype)
    blocks = []
    place = 0
    for first in range(-3, 4):
        for second in range(-3, 4):
            for third in range(-3, 4):
                if max(abs(first), abs(second), abs(third)) >= 2:
                    blocks.append(transfer_weight[place])
                    place = place + 1
                else:
                    blocks.append(empty)
    grid = jnp.stack(blocks).reshape(7, 7, 7, coeffs, coeffs)
    rows = []
    for source in range(8):
        columns = []
        for target in range(8):
            starts = [((source >> (2 - coord)) & 1) - ((target >> (2 - coord)) & 1) + 1 for coord in range(3)]
            piece = grid[starts[0]:starts[0] + 5:2, starts[1]:starts[1] + 5:2, starts[2]:starts[2] + 5:2]
            columns.append(piece.reshape(27, coeffs, coeffs))
        rows.append(jnp.concatenate(columns, axis=2))
    return jnp.concatenate(rows, axis=1)


def translate(padded, kernels, extent):
    size_x, size_y, size_z = extent
    group_width = padded.shape[3]
    row_count = size_x * size_y * size_z

    def one_offset(position, running):
        position = jnp.asarray(position).astype(jnp.int32)
        shift_x = position // 9
        shift_y = (position // 3) % 3
        shift_z = position % 3
        source = lax.dynamic_slice(padded, (shift_x, shift_y, shift_z, shift_x * 0), (size_x, size_y, size_z, group_width))
        kernel = lax.dynamic_index_in_dim(kernels, position, 0, keepdims=False)
        return running + jnp.dot(source.reshape(row_count, group_width), kernel, preferred_element_type=jnp.float32)

    running = lax.fori_loop(0, 27, one_offset, jnp.zeros((row_count, group_width), jnp.float32))
    return running.reshape(size_x, size_y, size_z, group_width)


def group_parents(boxes):
    size_x, size_y, size_z, coeffs = boxes.shape
    unpacked = boxes.reshape(size_x // 2, 2, size_y // 2, 2, size_z // 2, 2, coeffs)
    return unpacked.transpose(0, 2, 4, 1, 3, 5, 6).reshape(size_x // 2, size_y // 2, size_z // 2, 8 * coeffs)


def spread_children(grouped):
    size_x, size_y, size_z, group_width = grouped.shape
    coeffs = group_width // 8
    unpacked = grouped.reshape(size_x, size_y, size_z, 2, 2, 2, coeffs)
    return unpacked.transpose(0, 3, 1, 4, 2, 5, 6).reshape(2 * size_x, 2 * size_y, 2 * size_z, coeffs)


def lift(grouped, upward_weight):
    leading = grouped.shape[:3]
    product = jnp.dot(grouped.reshape(-1, grouped.shape[3]), upward_weight, preferred_element_type=jnp.float32)
    return product.astype(jnp.bfloat16).reshape(leading + (upward_weight.shape[1],))


def descend(boxes, downward_weight):
    leading = boxes.shape[:3]
    product = jnp.dot(boxes.astype(jnp.bfloat16).reshape(-1, boxes.shape[3]), downward_weight, preferred_element_type=jnp.float32)
    return product.reshape(leading + (downward_weight.shape[1],))


def padded_once(grouped):
    return jnp.pad(grouped, ((1, 1), (1, 1), (1, 1), (0, 0)))


def reference(densities, upward_weight, transfer_weight, downward_weight):
    kernels = kernel_table(transfer_weight)
    far_leaf = translate(padded_once(densities), kernels, densities.shape[:3])
    middle_group = group_parents(lift(densities, upward_weight))
    far_middle = translate(padded_once(middle_group), kernels, middle_group.shape[:3])
    top_group = group_parents(lift(middle_group, upward_weight))
    far_top = translate(padded_once(top_group), kernels, top_group.shape[:3])
    local_top = spread_children(far_top)
    local_middle = far_middle + descend(local_top, downward_weight)
    return far_leaf + descend(spread_children(local_middle), downward_weight)
```

```python
import functools

import jax
import jax.numpy as jnp
from jax import lax
from jax.experimental import pallas as pl
from jax.experimental.pallas import tpu as pltpu
from jax.sharding import PartitionSpec as P

BF = jnp.bfloat16
F32 = jnp.float32
WHOLE = pl.BlockSpec(memory_space=pltpu.VMEM)


def params(mib):
    return pltpu.CompilerParams(vmem_limit_bytes=mib * 2**20)


def exchange(low, high, axis):
    count = lax.axis_size(axis)
    odd = lax.axis_index(axis) % 2 == 1

    def swap(block, first):
        pairs = []
        for i in range(first, count - 1, 2):
            pairs += [(i, i + 1), (i + 1, i)]
        return lax.ppermute(block, axis, pairs)

    got = swap(jnp.where(odd, low, high), 0)
    if count > 2:
        other = swap(jnp.where(odd, high, low), 1)
    else:
        other = jnp.zeros_like(got)
    return jnp.where(odd, got, other), jnp.where(odd, other, got)


def lift_kernel(base, weight, middle, top):
    size_y, size_z, size_x, width = base.shape
    half, part = size_x // 2, size_x // 4
    coeffs = weight.shape[1]
    up = weight[...]

    def lift(rows):
        return jnp.dot(rows, up, preferred_element_type=F32).astype(BF).astype(F32)

    boxes = {}
    for y in range(size_y):
        for z in range(size_z):
            boxes[y, z] = lift(base[y, z])
    coarse = {}
    for y in range(size_y // 2):
        for z in range(size_z // 2):
            pieces = []
            for u in range(2):
                for v in range(2):
                    for w in range(2):
                        pieces.append(boxes[2 * y + v, 2 * z + w][u * half : (u + 1) * half])
            group = jnp.concatenate(pieces, axis=1).astype(BF)
            middle[y, z] = group
            coarse[y, z] = lift(group)
    for y in range(size_y // 4):
        for z in range(size_z // 4):
            pieces = []
            for u in range(2):
                for v in range(2):
                    for w in range(2):
                        pieces.append(coarse[2 * y + v, 2 * z + w][u * part : (u + 1) * part])
            group = jnp.concatenate(pieces, axis=1)
            top[y, z] = jnp.concatenate([group, jnp.zeros_like(group)], axis=0).astype(BF)


def lifted(base, upward_weight):
    size_y, size_z, size_x, width = base.shape
    return pl.pallas_call(
        lift_kernel,
        out_shape=(
            jax.ShapeDtypeStruct((size_y // 2, size_z // 2, size_x // 2, width), BF),
            jax.ShapeDtypeStruct((size_y // 4, size_z // 4, size_x // 2, width), BF),
        ),
        in_specs=[WHOLE, WHOLE],
        out_specs=(WHOLE, WHOLE),
        compiler_params=params(40),
        name="lift",
    )(base, upward_weight)


def table_kernel(weight, table):
    coeffs = weight.shape[1]

    def one(position, carry):
        first = position // 7
        second = position % 7
        mid_first = jnp.logical_and(first >= 2, first <= 4)
        mid = jnp.logical_and(mid_first, jnp.logical_and(second >= 2, second <= 4))
        skipped = 9 * jnp.clip(first - 2, 0, 3) + jnp.where(
            mid_first, 3 * jnp.clip(second - 2, 0, 3), 0
        )
        start = 7 * position - skipped
        blocks = []
        for third in range(7):
            if third in (2, 3, 4):
                place = jnp.where(mid, 0, start + third)
                block = weight[place].astype(F32)
                block = jnp.where(mid, jnp.zeros_like(block), block)
            else:
                place = start + third - jnp.where(mid, min(max(third - 2, 0), 3), 0)
                block = weight[place].astype(F32)
            blocks.append(block)
        for third in range(3):
            rows = [
                jnp.concatenate([blocks[2 * third + s + 1], blocks[2 * third + s]], axis=1)
                for s in range(2)
            ]
            table[first, second, third] = jnp.concatenate(rows, axis=0).astype(BF)
        return carry

    lax.fori_loop(0, 49, one, 0)


def tabled(transfer_weight):
    coeffs = transfer_weight.shape[1]
    return pl.pallas_call(
        table_kernel,
        out_shape=jax.ShapeDtypeStruct((7, 7, 3, 2 * coeffs, 2 * coeffs), BF),
        in_specs=[WHOLE],
        out_specs=WHOLE,
        compiler_params=params(40),
        name="table",
    )(transfer_weight)


def far_kernel(
    table, leaf, leaf_x, middle, middle_x, top, top_x, down, out,
    leaf_lo, leaf_hi, middle_lo, middle_hi, top_lo, top_hi, kernels, total,
):
    size_y, size_z = leaf.shape[0] - 2, leaf.shape[1] - 2
    size_x, width = leaf.shape[2:]
    half, part = size_x // 2, size_x // 4
    coeffs = width // 8
    pair = 2 * coeffs

    def after(rows, last):
        return jnp.concatenate([rows[1:], last], axis=0)

    def before(rows, first):
        return jnp.concatenate([first, rows[:-1]], axis=0)

    def move_leaf(position, carry):
        y, z = position // (size_z + 2), position % (size_z + 2)
        rows = leaf[y, z].astype(F32)
        low, high = leaf_x[0, pl.ds(position, 1)], leaf_x[1, pl.ds(position, 1)]
        q = [rows[i * part : (i + 1) * part] for i in range(4)]
        leaf_lo[y, z] = jnp.concatenate([before(q[3], low), q[2], q[0], q[1]], axis=0).astype(BF)
        leaf_hi[y, z] = jnp.concatenate([q[2], q[3], q[1], after(q[0], high)], axis=0).astype(BF)
        return carry

    lax.fori_loop(0, (size_y + 2) * (size_z + 2), move_leaf, 0)
    wide = middle.shape[1]
    for y in range(middle.shape[0]):
        for z in range(wide):
            rows = middle[y, z].astype(F32)
            at = y * wide + z
            low, high = middle_x[0, at : at + 1], middle_x[1, at : at + 1]
            q = [rows[:part], rows[part:]]
            middle_lo[y, z] = jnp.concatenate([before(q[1], low), q[0]], axis=0).astype(BF)
            middle_hi[y, z] = jnp.concatenate([q[1], after(q[0], high)], axis=0).astype(BF)
    wide = top.shape[1]
    for y in range(top.shape[0]):
        for z in range(wide):
            rows = top[y, z].astype(F32)[:part]
            at = y * wide + z
            low, high = top_x[0, at : at + 1], top_x[1, at : at + 1]
            none = jnp.zeros_like(rows)
            top_lo[y, z] = jnp.concatenate([before(rows, low), none], axis=0).astype(BF)
            top_hi[y, z] = jnp.concatenate([after(rows, high), none], axis=0).astype(BF)

    leaves = (leaf_lo, leaf, leaf_hi)
    middles = (middle_lo, middle, middle_hi)
    tops = (top_lo, top, top_hi)
    leaf_rows = size_y * size_z * size_x
    step = 2 * size_z * size_x
    slot = 0
    for dx in range(3):
        for dy in range(3):
            for dz in range(3):
                if (dx, dy, dz) == (1, 1, 1):
                    continue
                for sx in range(2):
                    for sy in range(2):
                        parts = [
                            table[2 * dx + sx - tx + 1, 2 * dy + sy - ty + 1, dz]
                            for tx in range(2)
                            for ty in range(2)
                        ]
                        at = (2 * sx + sy) * pair
                        kernels[slot, at : at + pair] = jnp.concatenate(parts, axis=1)
                kernel = kernels[slot]
                first = slot == 0

                def add(rows, at):
                    product = jnp.dot(rows, kernel, preferred_element_type=F32)
                    where = slice(at, at + rows.shape[0])
                    total[where] = product if first else total[where] + product

                for y in range(0, size_y, 2):
                    rows = leaves[dx][y + dy : y + dy + 2, dz : dz + size_z]
                    add(rows.reshape(step, width), y // 2 * step)
                rows = [
                    middles[dx][dy : dy + size_y // 2, dz : dz + size_z // 2].reshape(-1, width),
                    tops[dx][dy : dy + size_y // 4, dz : dz + size_z // 4].reshape(-1, width),
                ]
                add(jnp.concatenate(rows, axis=0), leaf_rows)
                slot += 1

    weight = down[...]

    def spread(values, rows):
        pieces = []
        for y in range(2 * values[0]):
            for z in range(2 * values[1]):
                for u in range(2):
                    octant = 4 * u + 2 * (y % 2) + z % 2
                    parent = values[2](y // 2, z // 2)
                    pieces.append(parent[:rows, octant * coeffs : (octant + 1) * coeffs])
        return jnp.concatenate(pieces, axis=0).astype(BF)

    middle_rows = leaf_rows // 8
    at_top = leaf_rows + middle_rows

    def top_of(y, z):
        at = at_top + (y * (size_z // 4) + z) * half
        return total[at : at + half]

    boxes = spread((size_y // 4, size_z // 4, top_of), part)
    local = total[leaf_rows:at_top] + jnp.dot(boxes, weight, preferred_element_type=F32)

    def middle_of(y, z):
        at = (y * (size_z // 2) + z) * half
        return local[at : at + half]

    boxes = spread((size_y // 2, size_z // 2, middle_of), half)
    out[...] = total[:leaf_rows] + jnp.dot(boxes, weight, preferred_element_type=F32)


def far(table, leaf, leaf_x, middle, middle_x, top, top_x, down):
    size_y, size_z = leaf.shape[0] - 2, leaf.shape[1] - 2
    size_x, width = leaf.shape[2:]
    rows = size_y * size_z * size_x
    more = rows // 8 + (size_y // 4) * (size_z // 4) * (size_x // 2)
    scratch = [pltpu.VMEM(a.shape, BF) for a in (leaf, leaf, middle, middle, top, top)]
    return pl.pallas_call(
        far_kernel,
        out_shape=jax.ShapeDtypeStruct((rows, width), F32),
        in_specs=[WHOLE] * 8,
        out_specs=WHOLE,
        scratch_shapes=scratch
        + [pltpu.VMEM((26, width, width), BF), pltpu.VMEM((rows + more, width), F32)],
        compiler_params=params(60),
        name="far",
    )(table, leaf, leaf_x, middle, middle_x, top, top_x, down)


def shards(densities, upward_weight, transfer_weight, downward_weight):
    size_x, size_y, size_z, width = densities.shape
    base = densities.reshape(size_x // 4, 2, 2, size_y, size_z, width)
    base = base.transpose(3, 4, 2, 1, 0, 5).reshape(size_y, size_z, size_x, width)
    middle, top = lifted(base, upward_weight)
    table = tabled(transfer_weight)
    levels = [base, middle, top]
    lasts = [size_x, size_x // 2, size_x // 4]

    def packed(pieces):
        return jnp.concatenate([piece.reshape(-1, width) for piece in pieces], axis=0)

    def unpacked(flat, shapes):
        pieces, at = [], 0
        for shape in shapes:
            count = shape[0] * shape[1] * (shape[2] if len(shape) > 2 else 1)
            pieces.append(flat[at : at + count].reshape(shape + (width,)))
            at += count
        return pieces

    low = packed([level[:, :, 0] for level in levels])
    high = packed([level[:, :, last - 1] for level, last in zip(levels, lasts)])
    shapes = [level.shape[:2] for level in levels]
    below, above = exchange(low, high, "gx")
    sides = [
        jnp.stack(both) for both in zip(unpacked(below, shapes), unpacked(above, shapes))
    ]

    def grown(arrays, dims, axis):
        def face(where):
            picked = []
            for array, dim in zip(arrays, dims):
                at = 0 if where == 0 else array.shape[dim] - 1
                picked.append(lax.slice_in_dim(array, at, at + 1, axis=dim))
            return picked

        shapes = [piece.shape[:-1] for piece in face(0)]
        rows = [piece.reshape(-1, width).shape[0] for piece in face(0)]
        below, above = exchange(packed(face(0)), packed(face(1)), axis)
        result, at = [], 0
        for array, dim, shape, count in zip(arrays, dims, shapes, rows):
            one = below[at : at + count].reshape(shape + (width,))
            two = above[at : at + count].reshape(shape + (width,))
            result.append(jnp.concatenate([one, array, two], axis=dim))
            at += count
        return result

    arrays = levels + sides
    arrays = grown(arrays, (1, 1, 1, 2, 2, 2), "gz")
    arrays = grown(arrays, (0, 0, 0, 1, 1, 1), "gy")
    levels, sides = arrays[:3], [side.reshape(2, -1, width).astype(F32) for side in arrays[3:]]
    result = far(
        table, levels[0], sides[0], levels[1], sides[1], levels[2], sides[2], downward_weight
    )
    result = result.reshape(size_y, size_z, 2, 2, size_x // 4, width)
    return result.transpose(4, 3, 2, 0, 1, 5).reshape(densities.shape)


def solution(mesh):
    placed = (P("gx", "gy", "gz", None), P(), P(), P())
    return jax.shard_map(
        shards, mesh=mesh, in_specs=placed, out_specs=P("gx", "gy", "gz", None), check_vma=False
    )
```

```python
import functools

import jax
import jax.numpy as jnp
from jax import lax
from jax.experimental import pallas as pl
from jax.experimental.pallas import tpu as pltpu
from jax.sharding import PartitionSpec as P

BF = jnp.bfloat16
F32 = jnp.float32
WHOLE = pl.BlockSpec(memory_space=pltpu.VMEM)


def params(mib):
    return pltpu.CompilerParams(vmem_limit_bytes=mib * 2**20)


def exchange(low, high, axis):
    count = lax.axis_size(axis)
    odd = lax.axis_index(axis) % 2 == 1

    def swap(block, first):
        pairs = []
        for i in range(first, count - 1, 2):
            pairs += [(i, i + 1), (i + 1, i)]
        return lax.ppermute(block, axis, pairs)

    got = swap(jnp.where(odd, low, high), 0)
    if count > 2:
        other = swap(jnp.where(odd, high, low), 1)
    else:
        other = jnp.zeros_like(got)
    return jnp.where(odd, got, other), jnp.where(odd, other, got)


def lift_kernel(base, weight, middle, top):
    size_y, size_z, size_x, width = base.shape
    half, part = size_x // 2, size_x // 4
    coeffs = weight.shape[1]
    up = weight[...]

    def lift(rows):
        return jnp.dot(rows, up, preferred_element_type=F32).astype(BF).astype(F32)

    boxes = {}
    for y in range(size_y):
        for z in range(size_z):
            boxes[y, z] = lift(base[y, z])
    coarse = {}
    for y in range(size_y // 2):
        for z in range(size_z // 2):
            pieces = []
            for u in range(2):
                for v in range(2):
                    for w in range(2):
                        pieces.append(boxes[2 * y + v, 2 * z + w][u * half : (u + 1) * half])
            group = jnp.concatenate(pieces, axis=1).astype(BF)
            middle[y, z] = group
            coarse[y, z] = lift(group)
    for y in range(size_y // 4):
        for z in range(size_z // 4):
            pieces = []
            for u in range(2):
                for v in range(2):
                    for w in range(2):
                        pieces.append(coarse[2 * y + v, 2 * z + w][u * part : (u + 1) * part])
            group = jnp.concatenate(pieces, axis=1)
            top[y, z] = jnp.concatenate([group, jnp.zeros_like(group)], axis=0).astype(BF)


def lifted(base, upward_weight):
    size_y, size_z, size_x, width = base.shape
    return pl.pallas_call(
        lift_kernel,
        out_shape=(
            jax.ShapeDtypeStruct((size_y // 2, size_z // 2, size_x // 2, width), BF),
            jax.ShapeDtypeStruct((size_y // 4, size_z // 4, size_x // 2, width), BF),
        ),
        in_specs=[WHOLE, WHOLE],
        out_specs=(WHOLE, WHOLE),
        compiler_params=params(40),
        name="lift",
    )(base, upward_weight)


def table_kernel(weight, table, blocks):
    coeffs, _, count = weight.shape
    lanes = 128

    def turn(source, carry):
        rows = weight[source].astype(F32)
        for at in range(0, count, lanes):
            part = rows[:, at : min(at + lanes, count)]
            if part.shape[1] < lanes:
                fill = jnp.zeros((coeffs, lanes - part.shape[1]), F32)
                part = jnp.concatenate([part, fill], axis=1)
            fill = jnp.zeros((lanes, lanes - coeffs), F32)
            turned = jnp.concatenate([part.T, fill], axis=1)
            blocks[pl.ds(at * coeffs + source, lanes, stride=coeffs), :] = turned
        return carry

    lax.fori_loop(0, coeffs, turn, 0, unroll=4)

    def one(position, carry):
        first = position // 7
        second = position % 7
        mid_first = jnp.logical_and(first >= 2, first <= 4)
        mid = jnp.logical_and(mid_first, jnp.logical_and(second >= 2, second <= 4))
        skipped = 9 * jnp.clip(first - 2, 0, 3) + jnp.where(
            mid_first, 3 * jnp.clip(second - 2, 0, 3), 0
        )
        start = 7 * position - skipped
        found = []
        for third in range(7):
            near = third in (2, 3, 4)
            if near:
                place = jnp.where(mid, 0, start + third)
            else:
                place = start + third - jnp.where(mid, min(max(third - 2, 0), 3), 0)
            block = blocks[pl.ds(pl.multiple_of(place * coeffs, 8), coeffs)]
            found.append(jnp.where(mid, 0.0, block) if near else block)
        moved = [pltpu.roll(block, coeffs, 1) for block in found[:6]]
        for third in range(3):
            rows = [found[2 * third + s + 1] + moved[2 * third + s] for s in range(2)]
            rows = jnp.concatenate(rows, axis=0)
            table[first, second, third] = rows[:, : 2 * coeffs].astype(BF)
        return carry

    lax.fori_loop(0, 49, one, 0, unroll=7)


def tabled(transfer_weight):
    count, coeffs, _ = transfer_weight.shape
    return pl.pallas_call(
        table_kernel,
        out_shape=jax.ShapeDtypeStruct((7, 7, 3, 2 * coeffs, 2 * coeffs), BF),
        in_specs=[WHOLE],
        out_specs=WHOLE,
        scratch_shapes=[pltpu.VMEM((-(-count // 128) * 128 * coeffs, 128), F32)],
        compiler_params=params(40),
        cost_estimate=pl.CostEstimate(flops=6 * 10**9, bytes_accessed=10**7, transcendentals=0),
        name="table",
    )(transfer_weight.transpose(1, 2, 0))


SHIFTS = [
    (dx, dy, dz)
    for dy in (1, 0, 2)
    for dz in (1, 0, 2)
    for dx in range(3)
    if (dx, dy, dz) != (1, 1, 1)
]


def moved_rows(rows, low, high):
    part = 8
    q = [rows[i : i + part] for i in range(0, rows.shape[0], part)]
    count = len(q)
    before = jnp.concatenate([low, q[-1][:-1]], axis=0)
    after = jnp.concatenate([q[0][1:], high], axis=0)
    if count == 4:
        return [before, q[2], q[0], q[1]], [q[2], q[3], q[1], after]
    if count == 2:
        return [before, q[0]], [q[1], after]
    return [before], [after]


def store_moved(rows, low, high, down, up, fill=False):
    rows = rows.astype(F32)
    one, two = moved_rows(rows, low, high)
    if fill:
        one, two = one + [jnp.zeros_like(rows)], two + [jnp.zeros_like(rows)]
    down[...] = jnp.concatenate(one, axis=0).astype(BF)
    up[...] = jnp.concatenate(two, axis=0).astype(BF)


def operator(table, shift, kernels, slot):
    dx, dy, dz = shift
    pair = table.shape[3]
    for sx in range(2):
        for sy in range(2):
            parts = [
                table[2 * dx + sx - tx + 1, 2 * dy + sy - ty + 1, dz]
                for tx in range(2)
                for ty in range(2)
            ]
            at = (2 * sx + sy) * pair
            kernels[slot, at : at + pair] = jnp.concatenate(parts, axis=1)
    return kernels[slot]


def near_kernel(table, leaf, below, above, out, leaf_lo, leaf_hi, kernels):
    size_y, size_z, size_x, width = leaf.shape
    low = below[: size_y * size_z].astype(F32)
    high = above[: size_y * size_z].astype(F32)
    for y in range(size_y):
        for z in range(size_z):
            at = y * size_z + z
            store_moved(
                leaf[y, z], low[at : at + 1], high[at : at + 1],
                leaf_lo.at[y, z], leaf_hi.at[y, z],
            )
    leaves = (leaf_lo, leaf, leaf_hi)
    for slot, (dx, dy, dz) in enumerate(SHIFTS):
        kernel = operator(table, (dx, dy, dz), kernels, slot)
        first_z, last_z = max(0, 1 - dz), size_z - max(0, dz - 1)
        first_y, last_y = max(0, 1 - dy), size_y - max(0, dy - 1)
        count = (last_z - first_z) * size_x
        for y in range(first_y, last_y, 2):
            many = min(2, last_y - y)
            rows = leaves[dx][
                y + dy - 1 : y + dy - 1 + many, first_z + dz - 1 : last_z + dz - 1
            ].reshape(many * count, width)
            product = jnp.dot(rows, kernel, preferred_element_type=F32)
            for i in range(many):
                at = ((y + i) * size_z + first_z) * size_x
                piece = product[i * count : (i + 1) * count]
                out[at : at + count] = piece if slot == 0 else out[at : at + count] + piece


def near(table, leaf, below, above):
    size_y, size_z, size_x, width = leaf.shape
    rows = size_y * size_z * size_x
    return pl.pallas_call(
        near_kernel,
        out_shape=jax.ShapeDtypeStruct((rows, width), F32),
        in_specs=[WHOLE] * 4,
        out_specs=WHOLE,
        scratch_shapes=[
            pltpu.VMEM(leaf.shape, BF),
            pltpu.VMEM(leaf.shape, BF),
            pltpu.VMEM((26, width, width), BF),
        ],
        compiler_params=params(60),
        cost_estimate=pl.CostEstimate(flops=10**10, bytes_accessed=10**7, transcendentals=0),
        name="near",
    )(table, leaf, below, above)


def far_kernel(
    total, table, middle, top, below_x, above_x, below_z, above_z, below_y, above_y, down, out,
    leaves, middles, tops, kernels, upper,
):
    size_y, size_z = 2 * middle.shape[0], 2 * middle.shape[1]
    half, width = middle.shape[2:]
    size_x = 2 * half
    coeffs = width // 8
    none = jnp.zeros((1, width), F32)

    sizes = [(size_y, size_z, size_x), (size_y // 2, size_z // 2, half), (size_y // 4, size_z // 4, half)]
    own = (None, middle, top)
    slabs = [{}, {}, {}]
    for side in range(2):
        x_block = (below_x, above_x)[side][...].astype(F32)
        z_block, y_block = (below_z, above_z)[side], (below_y, above_y)[side]
        at_x = at_z = at_y = 0
        for level, (count_y, count_z, rows) in enumerate(sizes):
            for y in range(count_y):
                if level > 0:
                    for z in range(count_z):
                        slabs[level].setdefault((y + 1, z + 1), [own[level][y, z], none, none])[
                            1 + side
                        ] = x_block[at_x + y * count_z + z : at_x + y * count_z + z + 1]
                slabs[level][y + 1, side * (count_z + 1)] = [
                    z_block[at_z + y * rows : at_z + (y + 1) * rows], none, none,
                ]
            for z in range(count_z + 2):
                slabs[level][side * (count_y + 1), z] = [
                    y_block[at_y + z * rows : at_y + (z + 1) * rows], none, none,
                ]
            at_x += count_y * count_z
            at_z += count_y * rows
            at_y += (count_z + 2) * rows
    for side in range(2):
        z_tail = (below_z, above_z)[side]
        y_tail = (below_y, above_y)[side]
        start_z = sum(c * r for c, _, r in sizes)
        start_y = sum((c + 2) * r for _, c, r in sizes)
        z_tail = z_tail[start_z:].astype(F32)
        y_tail = y_tail[start_y:].astype(F32)
        at_z = at_y = 0
        for level, (count_y, count_z, rows) in enumerate(sizes):
            for end in range(2):
                for y in range(count_y):
                    slabs[level][y + 1, side * (count_z + 1)][1 + end] = z_tail[at_z : at_z + 1]
                    at_z += 1
                for z in range(count_z + 2):
                    slabs[level][side * (count_y + 1), z][1 + end] = y_tail[at_y : at_y + 1]
                    at_y += 1

    copies = (leaves, middles, tops)
    for level in range(3):
        for (y, z), (rows, low, high) in slabs[level].items():
            copy = copies[level]
            copy[1, y, z] = rows
            if level == 2:
                rows = rows[: half // 2]
            store_moved(rows, low, high, copy.at[0, y, z], copy.at[2, y, z], level == 2)

    leaf_rows = size_y * size_z * size_x
    out[...] = total[...]
    for slot, (dx, dy, dz) in enumerate(SHIFTS):
        kernel = operator(table, (dx, dy, dz), kernels, slot)
        places, rows = [], []
        for y in range(size_y):
            for z in range(size_z):
                if y + dy in (0, size_y + 1) or z + dz in (0, size_z + 1):
                    places.append((y * size_z + z) * size_x)
                    rows.append(leaves[dx, y + dy, z + dz])
        rows += [
            middles[dx, dy : dy + size_y // 2, dz : dz + size_z // 2].reshape(-1, width),
            tops[dx, dy : dy + size_y // 4, dz : dz + size_z // 4].reshape(-1, width),
        ]
        product = jnp.dot(jnp.concatenate(rows, axis=0), kernel, preferred_element_type=F32)
        for i, at in enumerate(places):
            out[at : at + size_x] += product[i * size_x : (i + 1) * size_x]
        rest = product[len(places) * size_x :]
        upper[...] = rest if slot == 0 else upper[...] + rest

    weight = down[...]

    def spread(count_y, count_z, parent, rows):
        pieces = []
        for y in range(2 * count_y):
            for z in range(2 * count_z):
                for u in range(2):
                    octant = 4 * u + 2 * (y % 2) + z % 2
                    values = parent(y // 2, z // 2)
                    pieces.append(values[:rows, octant * coeffs : (octant + 1) * coeffs])
        return jnp.concatenate(pieces, axis=0).astype(BF)

    middle_rows = leaf_rows // 8

    def top_of(y, z):
        at = middle_rows + (y * (size_z // 4) + z) * half
        return upper[at : at + half]

    boxes = spread(size_y // 4, size_z // 4, top_of, half // 2)
    local = upper[:middle_rows] + jnp.dot(boxes, weight, preferred_element_type=F32)

    def middle_of(y, z):
        at = (y * (size_z // 2) + z) * half
        return local[at : at + half]

    boxes = spread(size_y // 2, size_z // 2, middle_of, half)
    out[...] += jnp.dot(boxes, weight, preferred_element_type=F32)


def far(total, table, middle, top, halos, down):
    width = total.shape[1]
    size_y, size_z, half = 2 * middle.shape[0], 2 * middle.shape[1], middle.shape[2]
    upper = half * ((size_y // 2) * (size_z // 2) + (size_y // 4) * (size_z // 4))
    return pl.pallas_call(
        far_kernel,
        out_shape=jax.ShapeDtypeStruct(total.shape, F32),
        in_specs=[WHOLE] * 11,
        out_specs=WHOLE,
        scratch_shapes=[
            pltpu.VMEM((3, size_y + 2, size_z + 2, 2 * half, width), BF),
            pltpu.VMEM((3, size_y // 2 + 2, size_z // 2 + 2, half, width), BF),
            pltpu.VMEM((3, size_y // 4 + 2, size_z // 4 + 2, half, width), BF),
            pltpu.VMEM((26, width, width), BF),
            pltpu.VMEM((upper, width), F32),
        ],
        compiler_params=params(60),
        name="far",
    )(total, table, middle, top, *halos, down)


def shards(densities, upward_weight, transfer_weight, downward_weight):
    size_x, size_y, size_z, width = densities.shape
    base = densities.reshape(size_x // 4, 2, 2, size_y, size_z, width)
    base = base.transpose(3, 4, 2, 1, 0, 5).reshape(size_y, size_z, size_x, width)
    middle, top = lifted(base, upward_weight)
    levels = [base, middle, top]
    lasts = [size_x, size_x // 2, size_x // 4]

    def packed(pieces):
        rows = jnp.concatenate([piece.reshape(-1, width) for piece in pieces], axis=0)
        return jnp.pad(rows, ((0, -rows.shape[0] % 16), (0, 0)))

    def unpacked(flat, shapes):
        pieces, at = [], 0
        for shape in shapes:
            count = 1
            for extent in shape:
                count *= extent
            pieces.append(flat[at : at + count].reshape(shape + (width,)))
            at += count
        return pieces

    low = packed([level[:, :, 0] for level in levels])
    high = packed([level[:, :, last - 1] for level, last in zip(levels, lasts)])
    below_x, above_x = exchange(low, high, "gx")
    shapes = [level.shape[:2] for level in levels]
    sides = [
        jnp.stack(both) for both in zip(unpacked(below_x, shapes), unpacked(above_x, shapes))
    ]

    low_z = [level[:, 0] for level in levels] + [side[:, :, 0] for side in sides]
    high_z = [level[:, -1] for level in levels] + [side[:, :, -1] for side in sides]
    shapes = [piece.shape[:-1] for piece in low_z]
    low_z, high_z = packed(low_z), packed(high_z)
    low_z, high_z, transfer_weight = lax.optimization_barrier((low_z, high_z, transfer_weight))
    table = tabled(transfer_weight)
    below_z, above_z = exchange(low_z, high_z, "gz")

    lows, highs = unpacked(below_z, shapes), unpacked(above_z, shapes)

    def face(at):
        rows = [
            jnp.concatenate([one[at][None], level[at], two[at][None]], axis=0)
            for one, level, two in zip(lows[:3], levels, highs[:3])
        ]
        rows += [
            jnp.concatenate([one[:, at, None], side[:, at], two[:, at, None]], axis=1)
            for one, side, two in zip(lows[3:], sides, highs[3:])
        ]
        return packed(rows)

    low_y, high_y = face(0), face(-1)
    low_y, high_y, table = lax.optimization_barrier((low_y, high_y, table))
    below_y, above_y = exchange(low_y, high_y, "gy")
    total = near(table, base, below_x, above_x)
    halos = (below_x, above_x, below_z, above_z, below_y, above_y)
    result = far(total, table, middle, top, halos, downward_weight)
    result = result.reshape(size_y, size_z, 2, 2, size_x // 4, width)
    return result.transpose(4, 3, 2, 0, 1, 5).reshape(densities.shape)


def solution(mesh):
    placed = (P("gx", "gy", "gz", None), P(), P(), P())
    return jax.shard_map(
        shards, mesh=mesh, in_specs=placed, out_specs=P("gx", "gy", "gz", None), check_vma=False
    )
```

```python
import functools

import jax
import jax.numpy as jnp
from jax import lax
from jax.experimental import pallas as pl
from jax.experimental.pallas import tpu as pltpu
from jax.sharding import PartitionSpec as P

BF = jnp.bfloat16
F32 = jnp.float32
ANYWHERE = pl.BlockSpec(memory_space=pl.ANY)
HBM = pl.BlockSpec(memory_space=pltpu.HBM)
WHOLE = pl.BlockSpec(memory_space=pltpu.VMEM)


def params(mib):
    return pltpu.CompilerParams(vmem_limit_bytes=mib * 2**20)


def rounds(axis):
    count = lax.axis_size(axis)
    return [[(i, i + 1) for i in range(first, count - 1, 2)] for first in (0, 1)]


def swapped(block, axis, pairs):
    both = pairs + [(two, one) for one, two in pairs]
    return lax.ppermute(block, axis, both) if pairs else jnp.zeros_like(block)


def is_odd(axis):
    return lax.axis_index(axis) % 2 == 1


def exchange(low, high, axis):
    odd = is_odd(axis)
    first, other = rounds(axis)
    got = swapped(jnp.where(odd, low, high), axis, first)
    return got, swapped(jnp.where(odd, high, low), axis, other)


def exchange_corners(faces, axis_y, axis_z):
    odd_y, odd_z = is_odd(axis_y), is_odd(axis_z)
    count_z = lax.axis_size(axis_z)
    result = []
    for round_y, pairs_y in enumerate(rounds(axis_y)):
        low_y, high_y = faces if round_y == 0 else faces[::-1]
        for round_z, pairs_z in enumerate(rounds(axis_z)):
            low = [jnp.where(odd_y, one, two) for one, two in zip(low_y, high_y)]
            low = low if round_z == 0 else low[::-1]
            pairs = []
            for one, two in pairs_y:
                for three, four in pairs_z:
                    pairs.append((one * count_z + three, two * count_z + four))
                    pairs.append((one * count_z + four, two * count_z + three))
            face = jnp.where(odd_z, low[0], low[1])
            result.append(swapped(face, (axis_y, axis_z), pairs))
    return jnp.stack(result).reshape(2, 2, *result[0].shape)


def lift_kernel(base, weight, middle, top):
    size_y, size_z, size_x, width = base.shape
    half, part = size_x // 2, size_x // 4
    coeffs = weight.shape[1]
    up = weight[...]

    def lift(rows):
        return jnp.dot(rows, up, preferred_element_type=F32).astype(BF).astype(F32)

    boxes = {}
    for y in range(size_y):
        for z in range(size_z):
            boxes[y, z] = lift(base[y, z])
    coarse = {}
    for y in range(size_y // 2):
        for z in range(size_z // 2):
            pieces = []
            for u in range(2):
                for v in range(2):
                    for w in range(2):
                        pieces.append(boxes[2 * y + v, 2 * z + w][u * half : (u + 1) * half])
            group = jnp.concatenate(pieces, axis=1).astype(BF)
            middle[y, z] = group
            coarse[y, z] = lift(group)
    for y in range(size_y // 4):
        for z in range(size_z // 4):
            pieces = []
            for u in range(2):
                for v in range(2):
                    for w in range(2):
                        pieces.append(coarse[2 * y + v, 2 * z + w][u * part : (u + 1) * part])
            group = jnp.concatenate(pieces, axis=1)
            top[y, z] = jnp.concatenate([group, jnp.zeros_like(group)], axis=0).astype(BF)


def lifted(base, upward_weight):
    size_y, size_z, size_x, width = base.shape
    return pl.pallas_call(
        lift_kernel,
        out_shape=(
            jax.ShapeDtypeStruct((size_y // 2, size_z // 2, size_x // 2, width), BF),
            jax.ShapeDtypeStruct((size_y // 4, size_z // 4, size_x // 2, width), BF),
        ),
        in_specs=[WHOLE, WHOLE],
        out_specs=(WHOLE, WHOLE),
        compiler_params=params(24),
        name="lift",
    )(base, upward_weight)


def fill_table(weight, arriving, table, blocks):
    coeffs, _, count = weight.shape
    lanes, batch = 128, coeffs // len(arriving)

    def turn(source, carry):
        rows = weight[source].astype(F32)
        for at in range(0, count, lanes):
            part = widened(rows[:, at : min(at + lanes, count)])
            turned = widened(part.T)
            blocks[pl.ds(at * coeffs + source, lanes, stride=coeffs), :] = turned
        return carry

    for i, copy in enumerate(arriving):
        copy.wait()
        lax.fori_loop(i * batch, (i + 1) * batch, turn, 0, unroll=4)

    def one(position, carry):
        first = position // 7
        second = position % 7
        mid_first = jnp.logical_and(first >= 2, first <= 4)
        mid = jnp.logical_and(mid_first, jnp.logical_and(second >= 2, second <= 4))
        skipped = 9 * jnp.clip(first - 2, 0, 3) + jnp.where(
            mid_first, 3 * jnp.clip(second - 2, 0, 3), 0
        )
        start = 7 * position - skipped
        found = []
        for third in range(7):
            near = third in (2, 3, 4)
            if near:
                place = jnp.where(mid, 0, start + third)
            else:
                place = start + third - jnp.where(mid, min(max(third - 2, 0), 3), 0)
            block = blocks[pl.ds(pl.multiple_of(place * coeffs, 8), coeffs)]
            found.append(jnp.where(mid, 0.0, block) if near else block)
        moved = [pltpu.roll(block, coeffs, 1) for block in found[:6]]
        for third in range(3):
            rows = [found[2 * third + s + 1] + moved[2 * third + s] for s in range(2)]
            rows = jnp.concatenate(rows, axis=0)
            table[third, first, second] = rows[:, : 2 * coeffs].astype(BF)
        return carry

    lax.fori_loop(0, 49, one, 0, unroll=7)


SLOTS = 8
SHIFTS = [
    (dx, dy, dz)
    for dz in (1, 0, 2)
    for dy in (1, 0, 2)
    for dx in range(3)
    if (dx, dy, dz) != (1, 1, 1)
]


def moved_rows(rows, low, high):
    part = 8
    q = [rows[i : i + part] for i in range(0, rows.shape[0], part)]
    count = len(q)
    before = jnp.concatenate([low, q[-1][:-1]], axis=0)
    after = jnp.concatenate([q[0][1:], high], axis=0)
    if count == 4:
        return [before, q[2], q[0], q[1]], [q[2], q[3], q[1], after]
    if count == 2:
        return [before, q[0]], [q[1], after]
    return [before], [after]


def widened(rows):
    fill = -rows.shape[1] % 128
    if fill:
        zeros = jnp.zeros((rows.shape[0], fill), rows.dtype)
        rows = jnp.concatenate([rows, zeros], axis=1)
    return rows


def store_moved(rows, low, high, copies, y, z, fill=False):
    rows = widened(rows.astype(F32))
    one, two = moved_rows(rows, widened(low), widened(high))
    three = [one, [rows], two]
    for dx in range(3):
        if fill:
            three[dx] = three[dx] + [jnp.zeros_like(rows)]
        copies[dx, y, z] = jnp.concatenate(three[dx], axis=0).astype(BF)


def operator(table, shift, kernels, slot):
    dx, dy, dz = shift
    slot = slot % kernels.shape[0]
    pair = table.shape[4]
    for sx in range(2):
        for sy in range(2):
            parts = [
                table[dz, 2 * dx + sx - tx + 1, 2 * dy + sy - ty + 1]
                for tx in range(2)
                for ty in range(2)
            ]
            at = (2 * sx + sy) * pair
            kernels[slot, at : at + pair] = widened(jnp.concatenate(parts, axis=1))
    rows = kernels.shape[1]
    if rows > 4 * pair:
        kernels[slot, 4 * pair :] = jnp.zeros((rows - 4 * pair, kernels.shape[2]), BF)
    return kernels[slot]


def add_near(slots, table, leaf, below, above, leaves, kernels, total, ready=None):
    size_y, size_z, size_x, width = leaf.shape
    low = below[: size_y * size_z].astype(F32)
    high = above[: size_y * size_z].astype(F32)
    for y in range(size_y):
        for z in range(size_z):
            at = y * size_z + z
            store_moved(leaf[y, z], low[at : at + 1], high[at : at + 1], leaves, y, z)
    if slots[0] > 0:
        total[...] = jnp.zeros_like(total)
    for slot in slots:
        dx, dy, dz = SHIFTS[slot]
        if ready is not None:
            ready(dz)
        kernel = operator(table, (dx, dy, dz), kernels, slot)
        first_z, last_z = max(0, 1 - dz), size_z - max(0, dz - 1)
        first_y, last_y = max(0, 1 - dy), size_y - max(0, dy - 1)
        count = (last_z - first_z) * size_x
        rows = leaves[
            dx, first_y + dy - 1 : last_y + dy - 1, first_z + dz - 1 : last_z + dz - 1
        ].reshape(-1, leaves.shape[4])
        product = jnp.dot(rows, kernel, preferred_element_type=F32)
        for i in range(last_y - first_y):
            at = ((first_y + i) * size_z + first_z) * size_x
            piece = product[i * count : (i + 1) * count]
            total[at : at + count] = piece if slot == 0 else total[at : at + count] + piece


def first_kernel(
    given, leaf, below, above, _, table, total, weight, blocks, leaves, kernels, arrived
):
    coeffs = given.shape[0]
    count = arrived.shape[0]
    batch = coeffs // count
    arriving = []
    for i in range(count):
        part = pl.ds(i * batch, batch)
        arriving.append(pltpu.make_async_copy(given.at[part], weight.at[part], arrived.at[i]))
        arriving[i].start()
    fill_table(weight, arriving, table, blocks)
    add_near(range(len(SHIFTS)), table, leaf, below, above, leaves, kernels, total)


def first_part(transfer_weight, leaf, below, above, after):
    count, coeffs, _ = transfer_weight.shape
    size_y, size_z, size_x, width = leaf.shape
    wide = -(-width // 128) * 128
    return pl.pallas_call(
        first_kernel,
        out_shape=(
            jax.ShapeDtypeStruct((3, 7, 7, 2 * coeffs, 2 * coeffs), BF),
            jax.ShapeDtypeStruct((size_y * size_z * size_x, wide), F32),
        ),
        in_specs=[HBM] + [WHOLE] * 3 + [ANYWHERE],
        out_specs=(WHOLE, WHOLE),
        scratch_shapes=[
            pltpu.VMEM((coeffs, coeffs, count), BF),
            pltpu.VMEM((-(-count // 128) * 128 * coeffs, 128), F32),
            pltpu.VMEM((3, size_y, size_z, size_x, wide), BF),
            pltpu.VMEM((SLOTS, wide, wide), BF),
            pltpu.SemaphoreType.DMA((7,)),
        ],
        compiler_params=params(32),
        cost_estimate=pl.CostEstimate(flops=2 * 10**10, bytes_accessed=10**7, transcendentals=0),
        name="first",
    )(transfer_weight.transpose(1, 2, 0), leaf, below, above, after)


def far_kernel(
    odd, near, table, middle, top, below_x, above_x, got_z, got_y, got_yz, down, out,
    total, leaves, middles, tops, kernels, upper, turned,
):
    size_y, size_z = 2 * middle.shape[0], 2 * middle.shape[1]
    half, width = middle.shape[2:]
    size_x = 2 * half
    coeffs = width // 8
    none = jnp.zeros((1, width), F32)
    odd_y, odd_z = odd[0] == 1, odd[1] == 1

    def chosen(is_odd, side, got, rows):
        first, other = got[0, rows], got[1, rows]
        pair = (first, other) if side == 0 else (other, first)
        return jnp.where(is_odd, pair[0], pair[1])

    def corner(side_y, side_z, rows):
        near_y = [chosen(odd_z, side_z, got_yz.at[i], rows) for i in range(2)]
        pair = near_y if side_y == 0 else near_y[::-1]
        return jnp.where(odd_y, pair[0], pair[1])

    sizes = [(size_y, size_z, size_x), (size_y // 2, size_z // 2, half), (size_y // 4, size_z // 4, half)]
    own = (None, middle, top)
    slabs = [{}, {}, {}]
    at_x = 0
    sides_x = [below_x[...].astype(F32), above_x[...].astype(F32)]
    for level, (count_y, count_z, rows) in enumerate(sizes):
        for y in range(count_y):
            for z in range(count_z):
                if level > 0:
                    ends = [side[at_x : at_x + 1] for side in sides_x]
                    slabs[level][y + 1, z + 1] = [own[level][y, z], *ends]
                at_x += 1

    def unpack(read, spots):
        at = 0
        for level, (_, _, rows) in enumerate(sizes):
            for spot in spots(level):
                slabs[level][spot] = [read(slice(at, at + rows))]
                at += rows
        count = 2 * sum(len(spots(level)) for level in range(3))
        tail = read(slice(at, at + -(-count // 16) * 16)).astype(F32)
        at = 0
        for level in range(3):
            for end in range(2):
                for spot in spots(level):
                    slabs[level][spot].append(tail[at : at + 1])
                    at += 1

    for side in range(2):
        unpack(
            functools.partial(chosen, odd_z, side, got_z),
            lambda level: [(y + 1, side * (sizes[level][1] + 1)) for y in range(sizes[level][0])],
        )
        unpack(
            functools.partial(chosen, odd_y, side, got_y),
            lambda level: [(side * (sizes[level][0] + 1), z + 1) for z in range(sizes[level][1])],
        )
        for other in range(2):
            unpack(
                functools.partial(corner, side, other),
                lambda level: [(side * (sizes[level][0] + 1), other * (sizes[level][1] + 1))],
            )

    copies = (leaves, middles, tops)
    for level in range(3):
        for (y, z), (rows, low, high) in slabs[level].items():
            if level == 2:
                rows = rows[: half // 2]
            store_moved(rows, low, high, copies[level], y, z, level == 2)

    total[...] = near[...]
    leaf_rows = size_y * size_z * size_x
    wide = kernels.shape[1]
    for slot, (dx, dy, dz) in enumerate(SHIFTS):
        kernel = operator(table, (dx, dy, dz), kernels, slot)
        places, rows = [], []
        for y in range(size_y):
            for z in range(size_z):
                if y + dy in (0, size_y + 1) or z + dz in (0, size_z + 1):
                    places.append((y * size_z + z) * size_x)
                    rows.append(leaves[dx, y + dy, z + dz])
        rows += [
            middles[dx, dy : dy + size_y // 2, dz : dz + size_z // 2].reshape(-1, wide),
            tops[dx, dy : dy + size_y // 4, dz : dz + size_z // 4].reshape(-1, wide),
        ]
        product = jnp.dot(jnp.concatenate(rows, axis=0), kernel, preferred_element_type=F32)
        for i, at in enumerate(places):
            total[at : at + size_x] += product[i * size_x : (i + 1) * size_x]
        rest = product[len(places) * size_x :, :width]
        upper[...] = rest if slot == 0 else upper[...] + rest

    weight = down[...]

    def spread(count_y, count_z, parent, rows):
        pieces = []
        for y in range(2 * count_y):
            for z in range(2 * count_z):
                for u in range(2):
                    octant = 4 * u + 2 * (y % 2) + z % 2
                    values = parent(y // 2, z // 2)
                    pieces.append(values[:rows, octant * coeffs : (octant + 1) * coeffs])
        return jnp.concatenate(pieces, axis=0).astype(BF)

    middle_rows = leaf_rows // 8

    def top_of(y, z):
        at = middle_rows + (y * (size_z // 4) + z) * half
        return upper[at : at + half]

    boxes = spread(size_y // 4, size_z // 4, top_of, half // 2)
    local = upper[:middle_rows] + jnp.dot(boxes, weight, preferred_element_type=F32)

    def middle_of(y, z):
        at = (y * (size_z // 2) + z) * half
        return local[at : at + half]

    boxes = spread(size_y // 2, size_z // 2, middle_of, half)
    product = jnp.dot(boxes, weight, preferred_element_type=F32)
    lanes = turned.shape[2]
    for y in range(size_y):
        for z in range(size_z):
            at = (y * size_z + z) * size_x
            part = slice(at, at + size_x)
            rows = total[part] + widened(product[part])
            for a in range(2):
                for b in range(2):
                    piece = rows[(2 * a + b) * 8 : (2 * a + b + 1) * 8]
                    start = ((2 * b + a) * size_y + y) * size_z + z
                    for c in range(wide // lanes):
                        turned[c, pl.ds(start, 8, stride=4 * size_y * size_z), :] = piece[
                            :, c * lanes : (c + 1) * lanes
                        ]
    def write(x, carry):
        for y in range(size_y):
            at = pl.ds((x * size_y + y) * size_z, size_z)
            rows = [turned[c, at] for c in range(wide // lanes)]
            out[x, y] = jnp.concatenate(rows, axis=1)[:, :width]
        return carry

    lax.fori_loop(0, size_x, write, 0, unroll=4)


def far(odd, near, table, middle, top, halos, down):
    rows, wide = near.shape
    width = middle.shape[3]
    size_y, size_z, half = 2 * middle.shape[0], 2 * middle.shape[1], middle.shape[2]
    upper = half * ((size_y // 2) * (size_z // 2) + (size_y // 4) * (size_z // 4))
    return pl.pallas_call(
        far_kernel,
        out_shape=jax.ShapeDtypeStruct((2 * half, size_y, size_z, width), F32),
        in_specs=[pl.BlockSpec(memory_space=pltpu.SMEM)] + [WHOLE] * 10,
        out_specs=WHOLE,
        scratch_shapes=[
            pltpu.VMEM((rows, wide), F32),
            pltpu.VMEM((3, size_y + 2, size_z + 2, 2 * half, wide), BF),
            pltpu.VMEM((3, size_y // 2 + 2, size_z // 2 + 2, half, wide), BF),
            pltpu.VMEM((3, size_y // 4 + 2, size_z // 4 + 2, half, wide), BF),
            pltpu.VMEM((SLOTS, wide, wide), BF),
            pltpu.VMEM((upper, width), F32),
            pltpu.VMEM((wide // 128, rows, 128), F32),
        ],
        compiler_params=params(32),
        name="far",
    )(odd, near, table, middle, top, *halos, down)


def shards(densities, upward_weight, transfer_weight, downward_weight):
    size_x, size_y, size_z, width = densities.shape
    base = densities.reshape(size_x // 4, 2, 2, size_y, size_z, width)
    base = base.transpose(3, 4, 2, 1, 0, 5).reshape(size_y, size_z, size_x, width)
    middle, top = lifted(base, upward_weight)
    levels = [base, middle, top]
    lasts = [size_x, size_x // 2, size_x // 4]

    def packed(pieces):
        rows = jnp.concatenate([piece.reshape(-1, width) for piece in pieces], axis=0)
        return jnp.pad(rows, ((0, -rows.shape[0] % 16), (0, 0)))

    def unpacked(flat, shapes):
        pieces, at = [], 0
        for shape in shapes:
            count = 1
            for extent in shape:
                count *= extent
            pieces.append(flat[at : at + count].reshape(shape + (width,)))
            at += count
        return pieces

    low = packed([level[:, :, 0] for level in levels])
    high = packed([level[:, :, last - 1] for level, last in zip(levels, lasts)])
    first, other = exchange(low, high, "gx")
    odd = is_odd("gx")
    below_x, above_x = jnp.where(odd, first, other), jnp.where(odd, other, first)
    shapes = [level.shape[:2] for level in levels]
    sides = [
        jnp.stack(both) for both in zip(unpacked(below_x, shapes), unpacked(above_x, shapes))
    ]

    def face_z(at):
        return packed([level[:, at] for level in levels] + [side[:, :, at] for side in sides])

    def face_y(at):
        return packed([level[at] for level in levels] + [side[:, at] for side in sides])

    def corner(at_y, at_z):
        rows = [level[at_y, at_z] for level in levels] + [side[:, at_y, at_z] for side in sides]
        return packed(rows)

    low_z = face_z(0)
    got_z = jnp.stack(exchange(low_z, face_z(-1), "gz"))
    got_y = jnp.stack(exchange(face_y(0), face_y(-1), "gy"))
    got_yz = exchange_corners([[corner(y, z) for z in (0, -1)] for y in (0, -1)], "gy", "gz")
    table, near = first_part(transfer_weight, base, below_x, above_x, low_z)
    odd = jnp.stack([is_odd("gy"), is_odd("gz")]).astype(jnp.int32)
    halos = (below_x, above_x, got_z, got_y, got_yz)
    return far(odd, near, table, middle, top, halos, downward_weight)


def solution(mesh):
    placed = (P("gx", "gy", "gz", None), P(), P(), P())
    return jax.shard_map(
        shards, mesh=mesh, in_specs=placed, out_specs=P("gx", "gy", "gz", None), check_vma=False
    )
```

```python
import functools

import jax
import jax.numpy as jnp
from jax import lax
from jax.experimental import pallas as pl
from jax.experimental.pallas import tpu as pltpu
from jax.sharding import PartitionSpec as P

BF = jnp.bfloat16
F32 = jnp.float32
ANYWHERE = pl.BlockSpec(memory_space=pl.ANY)
HBM = pl.BlockSpec(memory_space=pltpu.HBM)
WHOLE = pl.BlockSpec(memory_space=pltpu.VMEM)


def params(mib):
    return pltpu.CompilerParams(vmem_limit_bytes=mib * 2**20)


def rounds(axis):
    count = lax.axis_size(axis)
    return [[(i, i + 1) for i in range(first, count - 1, 2)] for first in (0, 1)]


def swapped(block, axis, pairs):
    both = pairs + [(two, one) for one, two in pairs]
    return lax.ppermute(block, axis, both) if pairs else jnp.zeros_like(block)


def is_odd(axis):
    return lax.axis_index(axis) % 2 == 1


def exchange(low, high, axis):
    odd = is_odd(axis)
    first, other = rounds(axis)
    got = swapped(jnp.where(odd, low, high), axis, first)
    return got, swapped(jnp.where(odd, high, low), axis, other)


def exchange_corners(faces, axis_y, axis_z):
    odd_y, odd_z = is_odd(axis_y), is_odd(axis_z)
    count_z = lax.axis_size(axis_z)
    result = []
    for round_y, pairs_y in enumerate(rounds(axis_y)):
        low_y, high_y = faces if round_y == 0 else faces[::-1]
        for round_z, pairs_z in enumerate(rounds(axis_z)):
            low = [jnp.where(odd_y, one, two) for one, two in zip(low_y, high_y)]
            low = low if round_z == 0 else low[::-1]
            pairs = []
            for one, two in pairs_y:
                for three, four in pairs_z:
                    pairs.append((one * count_z + three, two * count_z + four))
                    pairs.append((one * count_z + four, two * count_z + three))
            face = jnp.where(odd_z, low[0], low[1])
            result.append(swapped(face, (axis_y, axis_z), pairs))
    return jnp.stack(result).reshape(2, 2, *result[0].shape)


def lift_kernel(base, weight, middle, top, low, high):
    size_y, size_z, size_x, width = base.shape
    half, part = size_x // 2, size_x // 4
    up = weight[...]

    def lift(rows):
        product = lax.dot_general(rows, up, (((1,), (1,)), ((), ())), preferred_element_type=F32)
        return product.astype(BF).astype(F32)

    lows, highs = [], []

    def ends(rows):
        lows.append(rows[:1])
        highs.append(rows[rows.shape[0] - 1 :])

    boxes = {}
    for y in range(size_y):
        for z in range(size_z):
            rows = base[y, z]
            boxes[y, z] = lift(rows)
            ends(rows.astype(F32))

    def grouped(boxes, y, z, rows):
        pieces = []
        for u in range(2):
            for v in range(2):
                for w in range(2):
                    pieces.append(boxes[2 * y + v, 2 * z + w][u * rows : (u + 1) * rows])
        return jnp.concatenate(pieces, axis=1)

    coarse = {}
    for y in range(size_y // 2):
        for z in range(size_z // 2):
            group = grouped(boxes, y, z, half)
            ends(group)
            middle[y, z] = group.astype(BF)
            coarse[y, z] = lift(group.astype(BF))
    for y in range(size_y // 4):
        for z in range(size_z // 4):
            group = grouped(coarse, y, z, part)
            ends(group)
            top[y, z] = jnp.concatenate([group, jnp.zeros_like(group)], axis=0).astype(BF)
    fill = [jnp.zeros((-len(lows) % 16, width), F32)]
    low[...] = jnp.concatenate(lows + fill, axis=0).astype(BF)
    high[...] = jnp.concatenate(highs + fill, axis=0).astype(BF)


def lifted(base, upward_weight):
    size_y, size_z, size_x, width = base.shape
    count = size_y * size_z + (size_y // 2) * (size_z // 2) + (size_y // 4) * (size_z // 4)
    ends = jax.ShapeDtypeStruct((-(-count // 16) * 16, width), BF)
    return pl.pallas_call(
        lift_kernel,
        out_shape=(
            jax.ShapeDtypeStruct((size_y // 2, size_z // 2, size_x // 2, width), BF),
            jax.ShapeDtypeStruct((size_y // 4, size_z // 4, size_x // 2, width), BF),
            ends,
            ends,
        ),
        in_specs=[WHOLE] * 2,
        out_specs=(WHOLE,) * 4,
        compiler_params=params(24),
        name="lift",
    )(base, upward_weight.T)


def turn_operators(weight, arriving, blocks):
    coeffs, _, count = weight.shape
    lanes, batch = 128, coeffs // len(arriving)

    def turn(source, carry):
        rows = weight[source].astype(F32)
        for at in range(0, count, lanes):
            part = widened(rows[:, at : min(at + lanes, count)])
            turned = widened(part.T)
            blocks[pl.ds(at * coeffs + source, lanes, stride=coeffs), :] = turned
        return carry

    for i, copy in enumerate(arriving):
        copy.wait()
        lax.fori_loop(i * batch, (i + 1) * batch, turn, 0, unroll=4)


def fill_entry(blocks, table, first, second, third, coeffs):
    def found(at):
        spot = (first, second, at)
        if all(2 <= i <= 4 for i in spot):
            return jnp.zeros((coeffs, blocks.shape[1]), F32)
        before = 0
        for i in range(spot[0] * 49 + spot[1] * 7 + at):
            before += not all(2 <= j <= 4 for j in (i // 49, i // 7 % 7, i % 7))
        return blocks[before * coeffs : (before + 1) * coeffs]

    rows = []
    for s in range(2):
        at = 2 * third + s
        rows.append(found(at + 1) + pltpu.roll(found(at), coeffs, 1))
    rows = jnp.concatenate(rows, axis=0)
    table[third, first, second] = rows[:, : 2 * coeffs].astype(BF)


SLOTS = 8
SHIFTS = [
    (dx, dy, dz)
    for dz in (1, 0, 2)
    for dy in (1, 0, 2)
    for dx in range(3)
    if (dx, dy, dz) != (1, 1, 1)
]


def moved_rows(rows, low, high):
    part = 8
    q = [rows[i : i + part] for i in range(0, rows.shape[0], part)]
    count = len(q)
    before = jnp.concatenate([low, q[-1][:-1]], axis=0)
    after = jnp.concatenate([q[0][1:], high], axis=0)
    if count == 4:
        return [before, q[2], q[0], q[1]], [q[2], q[3], q[1], after]
    if count == 2:
        return [before, q[0]], [q[1], after]
    return [before], [after]


def widened(rows):
    fill = -rows.shape[1] % 128
    if fill:
        zeros = jnp.zeros((rows.shape[0], fill), rows.dtype)
        rows = jnp.concatenate([rows, zeros], axis=1)
    return rows


def store_moved(rows, low, high, copies, y, z, fill=False):
    rows = widened(rows.astype(F32))
    one, two = moved_rows(rows, widened(low), widened(high))
    three = [one, [rows], two]
    for dx in range(3):
        if fill:
            three[dx] = three[dx] + [jnp.zeros_like(rows)]
        copies[dx, y, z] = jnp.concatenate(three[dx], axis=0).astype(BF)


def operator(table, shift, kernels, slot):
    dx, dy, dz = shift
    slot = slot % kernels.shape[0]
    pair = table.shape[4]
    for sx in range(2):
        for sy in range(2):
            parts = [
                table[dz, 2 * dx + sx - tx + 1, 2 * dy + sy - ty + 1]
                for tx in range(2)
                for ty in range(2)
            ]
            at = (2 * sx + sy) * pair
            kernels[slot, at : at + pair] = widened(jnp.concatenate(parts, axis=1))
    rows = kernels.shape[1]
    if rows > 4 * pair:
        kernels[slot, 4 * pair :] = jnp.zeros((rows - 4 * pair, kernels.shape[2]), BF)
    return kernels[slot]


def add_near(prepare, table, leaf, below, above, leaves, kernels, total):
    size_y, size_z, size_x, width = leaf.shape
    low = below[: size_y * size_z].astype(F32)
    high = above[: size_y * size_z].astype(F32)
    for y in range(size_y):
        for z in range(size_z):
            at = y * size_z + z
            store_moved(leaf[y, z], low[at : at + 1], high[at : at + 1], leaves, y, z)
    for slot, (dx, dy, dz) in enumerate(SHIFTS):
        prepare(dx, dy, dz)
        kernel = operator(table, (dx, dy, dz), kernels, slot)
        first_z, last_z = max(0, 1 - dz), size_z - max(0, dz - 1)
        first_y, last_y = max(0, 1 - dy), size_y - max(0, dy - 1)
        count = (last_z - first_z) * size_x
        rows = leaves[
            dx, first_y + dy - 1 : last_y + dy - 1, first_z + dz - 1 : last_z + dz - 1
        ].reshape(-1, leaves.shape[4])
        product = jnp.dot(rows, kernel, preferred_element_type=F32)
        for i in range(last_y - first_y):
            at = ((first_y + i) * size_z + first_z) * size_x
            piece = product[i * count : (i + 1) * count]
            total[at : at + count] = piece if slot == 0 else total[at : at + count] + piece


def first_kernel(
    given, leaf, below, above, _, table, total, weight, blocks, leaves, kernels, arrived
):
    coeffs = given.shape[0]
    count = arrived.shape[0]
    batch = coeffs // count
    arriving = []
    for i in range(count):
        part = pl.ds(i * batch, batch)
        arriving.append(pltpu.make_async_copy(given.at[part], weight.at[part], arrived.at[i]))
        arriving[i].start()
    turn_operators(weight, arriving, blocks)
    done = set()

    def prepare(dx, dy, dz):
        for first in range(2 * dx, 2 * dx + 3):
            for second in range(2 * dy, 2 * dy + 3):
                if (dz, first, second) not in done:
                    done.add((dz, first, second))
                    fill_entry(blocks, table, first, second, dz, coeffs)

    add_near(prepare, table, leaf, below, above, leaves, kernels, total)
    for dx, dy, dz in [(dx, dy, dz) for dx in range(3) for dy in range(3) for dz in range(3)]:
        prepare(dx, dy, dz)


def first_part(transfer_weight, leaf, below, above, after):
    count, coeffs, _ = transfer_weight.shape
    size_y, size_z, size_x, width = leaf.shape
    wide = -(-width // 128) * 128
    return pl.pallas_call(
        first_kernel,
        out_shape=(
            jax.ShapeDtypeStruct((3, 7, 7, 2 * coeffs, 2 * coeffs), BF),
            jax.ShapeDtypeStruct((size_y * size_z * size_x, wide), F32),
        ),
        in_specs=[HBM] + [WHOLE] * 3 + [ANYWHERE],
        out_specs=(WHOLE, WHOLE),
        scratch_shapes=[
            pltpu.VMEM((coeffs, coeffs, count), BF),
            pltpu.VMEM((-(-count // 128) * 128 * coeffs, 128), F32),
            pltpu.VMEM((3, size_y, size_z, size_x, wide), BF),
            pltpu.VMEM((SLOTS, wide, wide), BF),
            pltpu.SemaphoreType.DMA((7,)),
        ],
        compiler_params=params(32),
        cost_estimate=pl.CostEstimate(flops=2 * 10**10, bytes_accessed=10**7, transcendentals=0),
        name="first",
    )(transfer_weight.transpose(1, 2, 0), leaf, below, above, after)


def far_kernel(
    odd, near, table, middle, top, below_x, above_x, got_z, got_y, got_yz, down, out,
    total, leaves, middles, tops, kernels, upper, out_rows, sent,
):
    size_y, size_z = 2 * middle.shape[0], 2 * middle.shape[1]
    half, width = middle.shape[2:]
    size_x = 2 * half
    coeffs = width // 8
    none = jnp.zeros((1, width), F32)
    odd_y, odd_z = odd[0] == 1, odd[1] == 1

    def chosen(is_odd, side, got, rows):
        first, other = got[0, rows], got[1, rows]
        pair = (first, other) if side == 0 else (other, first)
        return jnp.where(is_odd, pair[0], pair[1])

    def corner(side_y, side_z, rows):
        near_y = [chosen(odd_z, side_z, got_yz.at[i], rows) for i in range(2)]
        pair = near_y if side_y == 0 else near_y[::-1]
        return jnp.where(odd_y, pair[0], pair[1])

    sizes = [(size_y, size_z, size_x), (size_y // 2, size_z // 2, half), (size_y // 4, size_z // 4, half)]
    own = (None, middle, top)
    slabs = [{}, {}, {}]
    at_x = 0
    sides_x = [below_x[...].astype(F32), above_x[...].astype(F32)]
    for level, (count_y, count_z, rows) in enumerate(sizes):
        for y in range(count_y):
            for z in range(count_z):
                if level > 0:
                    ends = [side[at_x : at_x + 1] for side in sides_x]
                    slabs[level][y + 1, z + 1] = [own[level][y, z], *ends]
                at_x += 1

    def unpack(read, spots):
        at = 0
        for level, (_, _, rows) in enumerate(sizes):
            for spot in spots(level):
                slabs[level][spot] = [read(slice(at, at + rows))]
                at += rows
        count = 2 * sum(len(spots(level)) for level in range(3))
        tail = read(slice(at, at + -(-count // 16) * 16)).astype(F32)
        at = 0
        for level in range(3):
            for end in range(2):
                for spot in spots(level):
                    slabs[level][spot].append(tail[at : at + 1])
                    at += 1

    for side in range(2):
        unpack(
            functools.partial(chosen, odd_z, side, got_z),
            lambda level: [(y + 1, side * (sizes[level][1] + 1)) for y in range(sizes[level][0])],
        )
        unpack(
            functools.partial(chosen, odd_y, side, got_y),
            lambda level: [(side * (sizes[level][0] + 1), z + 1) for z in range(sizes[level][1])],
        )
        for other in range(2):
            unpack(
                functools.partial(corner, side, other),
                lambda level: [(side * (sizes[level][0] + 1), other * (sizes[level][1] + 1))],
            )

    copies = (leaves, middles, tops)
    for level in range(3):
        for (y, z), (rows, low, high) in slabs[level].items():
            if level == 2:
                rows = rows[: half // 2]
            store_moved(rows, low, high, copies[level], y, z, level == 2)

    leaf_rows = size_y * size_z * size_x
    wide = kernels.shape[1]
    made = []
    for slot, (dx, dy, dz) in enumerate(SHIFTS):
        made.append(operator(table, (dx, dy, dz), kernels, slot))
        rows = [
            middles[dx, dy : dy + size_y // 2, dz : dz + size_z // 2].reshape(-1, wide),
            tops[dx, dy : dy + size_y // 4, dz : dz + size_z // 4].reshape(-1, wide),
        ]
        rows = jnp.concatenate(rows, axis=0)
        product = jnp.dot(rows, made[slot], preferred_element_type=F32)[:, :width]
        upper[...] = product if slot == 0 else upper[...] + product

    weight = down[...]

    def spread(count_y, count_z, parent, rows):
        pieces = []
        for y in range(2 * count_y):
            for z in range(2 * count_z):
                for u in range(2):
                    octant = 4 * u + 2 * (y % 2) + z % 2
                    values = parent(y // 2, z // 2)
                    pieces.append(values[:rows, octant * coeffs : (octant + 1) * coeffs])
        return jnp.concatenate(pieces, axis=0).astype(BF)

    middle_rows = leaf_rows // 8

    def top_of(y, z):
        at = middle_rows + (y * (size_z // 4) + z) * half
        return upper[at : at + half]

    boxes = spread(size_y // 4, size_z // 4, top_of, half // 2)
    local = upper[:middle_rows] + jnp.dot(boxes, weight, preferred_element_type=F32)

    def middle_of(y, z):
        at = (y * (size_z // 2) + z) * half
        return local[at : at + half]

    boxes = spread(size_y // 2, size_z // 2, middle_of, half)
    part_x = half // 2
    step = size_z * size_x
    touched = set()

    def finish(y):
        part = slice(y * step, (y + 1) * step)
        product = []

        def add(z):
            if not product:
                product.append(jnp.dot(boxes[part], weight, preferred_element_type=F32))
            at = z * size_x
            here = slice(y * step + at, y * step + at + size_x)
            source = total if here.start in touched else near
            rows = source[here] + widened(product[0][at : at + size_x])
            for i in range(size_x):
                a, b, x = i // half, i // part_x % 2, i % part_x
                out_rows[4 * x + 2 * b + a, y, z : z + 1] = rows[i : i + 1, :width]

        return [functools.partial(add, z) for z in range(size_z)]

    leaving = []

    def leave(ys):
        rows = pl.ds(ys.start, len(ys))
        copy = pltpu.make_async_copy(out_rows.at[:, rows], out.at[:, rows], sent.at[len(leaving)])
        copy.start()
        leaving.append(copy)

    steps = []
    halves = [range(0, size_y // 2), range(size_y // 2, size_y)]
    for ys in halves:
        count = -(-len(steps) // (len(SHIFTS) - 2))
        for slot, (dx, dy, dz) in enumerate(SHIFTS):
            places, rows = [], []
            for y in ys:
                for z in range(size_z):
                    if y + dy in (0, size_y + 1) or z + dz in (0, size_z + 1):
                        places.append((y * size_z + z) * size_x)
                        rows.append(leaves[dx, y + dy, z + dz])
            if rows:
                rows = jnp.concatenate(rows, axis=0)
                product = jnp.dot(rows, kernels[slot], preferred_element_type=F32)
                for i, at in enumerate(places):
                    source = total if at in touched else near
                    touched.add(at)
                    total[at : at + size_x] = (
                        source[at : at + size_x] + product[i * size_x : (i + 1) * size_x]
                    )
            for one in steps[:count]:
                one()
            steps = steps[count:]
        assert not steps
        if ys is not halves[0]:
            leave(halves[0])
        steps = [one for y in ys for one in finish(y)]
    for one in steps:
        one()
    leave(halves[1])
    for copy in leaving:
        copy.wait()


def far(odd, near, table, middle, top, halos, down):
    rows, wide = near.shape
    width = middle.shape[3]
    size_y, size_z, half = 2 * middle.shape[0], 2 * middle.shape[1], middle.shape[2]
    upper = half * ((size_y // 2) * (size_z // 2) + (size_y // 4) * (size_z // 4))
    return pl.pallas_call(
        far_kernel,
        out_shape=jax.ShapeDtypeStruct((2 * half, size_y, size_z, width), F32),
        in_specs=[pl.BlockSpec(memory_space=pltpu.SMEM)] + [WHOLE] * 10,
        out_specs=HBM,
        scratch_shapes=[
            pltpu.VMEM((rows, wide), F32),
            pltpu.VMEM((3, size_y + 2, size_z + 2, 2 * half, wide), BF),
            pltpu.VMEM((3, size_y // 2 + 2, size_z // 2 + 2, half, wide), BF),
            pltpu.VMEM((3, size_y // 4 + 2, size_z // 4 + 2, half, wide), BF),
            pltpu.VMEM((len(SHIFTS), wide, wide), BF),
            pltpu.VMEM((upper, width), F32),
            pltpu.VMEM((2 * half, size_y, size_z, width), F32),
            pltpu.SemaphoreType.DMA((2,)),
        ],
        compiler_params=params(42),
        name="far",
    )(odd, near, table, middle, top, *halos, down)


def shards(densities, upward_weight, transfer_weight, downward_weight):
    size_x, size_y, size_z, width = densities.shape
    base = densities.reshape(size_x // 4, 2, 2, size_y, size_z, width)
    base = base.transpose(3, 4, 2, 1, 0, 5).reshape(size_y, size_z, size_x, width)
    middle, top, low, high = lifted(base, upward_weight)
    levels = [base, middle, top]

    def packed(pieces):
        rows = jnp.concatenate([piece.reshape(-1, width) for piece in pieces], axis=0)
        return jnp.pad(rows, ((0, -rows.shape[0] % 16), (0, 0)))

    def unpacked(flat, shapes):
        pieces, at = [], 0
        for shape in shapes:
            count = 1
            for extent in shape:
                count *= extent
            pieces.append(flat[at : at + count].reshape(shape + (width,)))
            at += count
        return pieces

    first, other = exchange(low, high, "gx")
    odd = is_odd("gx")
    below_x, above_x = jnp.where(odd, first, other), jnp.where(odd, other, first)
    shapes = [level.shape[:2] for level in levels]
    sides = [
        jnp.stack(both) for both in zip(unpacked(below_x, shapes), unpacked(above_x, shapes))
    ]

    def face_z(at):
        return packed([level[:, at] for level in levels] + [side[:, :, at] for side in sides])

    def face_y(at):
        return packed([level[at] for level in levels] + [side[:, at] for side in sides])

    def corner(at_y, at_z):
        rows = [level[at_y, at_z] for level in levels] + [side[:, at_y, at_z] for side in sides]
        return packed(rows)

    low_z = face_z(0)
    got_z = jnp.stack(exchange(low_z, face_z(-1), "gz"))
    got_y = jnp.stack(exchange(face_y(0), face_y(-1), "gy"))
    got_yz = exchange_corners([[corner(y, z) for z in (0, -1)] for y in (0, -1)], "gy", "gz")
    table, near = first_part(transfer_weight, base, below_x, above_x, low_z)
    odd = jnp.stack([is_odd("gy"), is_odd("gz")]).astype(jnp.int32)
    halos = (below_x, above_x, got_z, got_y, got_yz)
    return far(odd, near, table, middle, top, halos, downward_weight)


def solution(mesh):
    placed = (P("gx", "gy", "gz", None), P(), P(), P())
    return jax.shard_map(
        shards, mesh=mesh, in_specs=placed, out_specs=P("gx", "gy", "gz", None), check_vma=False
    )
```

```python
import functools

import jax
import jax.numpy as jnp
from jax import lax
from jax.experimental import pallas as pl
from jax.experimental.pallas import tpu as pltpu
from jax.sharding import PartitionSpec as P

BF = jnp.bfloat16
F32 = jnp.float32
ANYWHERE = pl.BlockSpec(memory_space=pl.ANY)
HBM = pl.BlockSpec(memory_space=pltpu.HBM)
WHOLE = pl.BlockSpec(memory_space=pltpu.VMEM)


def params(mib):
    return pltpu.CompilerParams(vmem_limit_bytes=mib * 2**20)


def rounds(axis):
    count = lax.axis_size(axis)
    return [[(i, i + 1) for i in range(first, count - 1, 2)] for first in (0, 1)]


def swapped(block, axis, pairs):
    both = pairs + [(two, one) for one, two in pairs]
    return lax.ppermute(block, axis, both) if pairs else jnp.zeros_like(block)


def is_odd(axis):
    return lax.axis_index(axis) % 2 == 1


def exchange(low, high, axis):
    odd = is_odd(axis)
    first, other = rounds(axis)
    got = swapped(jnp.where(odd, low, high), axis, first)
    return got, swapped(jnp.where(odd, high, low), axis, other)


def exchange_corners(faces, axis_y, axis_z):
    odd_y, odd_z = is_odd(axis_y), is_odd(axis_z)
    count_z = lax.axis_size(axis_z)
    result = []
    for round_y, pairs_y in enumerate(rounds(axis_y)):
        low_y, high_y = faces if round_y == 0 else faces[::-1]
        for round_z, pairs_z in enumerate(rounds(axis_z)):
            low = [jnp.where(odd_y, one, two) for one, two in zip(low_y, high_y)]
            low = low if round_z == 0 else low[::-1]
            pairs = []
            for one, two in pairs_y:
                for three, four in pairs_z:
                    pairs.append((one * count_z + three, two * count_z + four))
                    pairs.append((one * count_z + four, two * count_z + three))
            face = jnp.where(odd_z, low[0], low[1])
            result.append(swapped(face, (axis_y, axis_z), pairs))
    return jnp.stack(result).reshape(2, 2, *result[0].shape)


def lift_kernel(base, weight, middle, top, low, high):
    size_y, size_z, size_x, width = base.shape
    half, part = size_x // 2, size_x // 4
    up = weight[: weight.shape[0] // 2][: width // 8]

    def lift(rows):
        product = lax.dot_general(rows, up, (((1,), (1,)), ((), ())), preferred_element_type=F32)
        return product.astype(BF).astype(F32)

    lows, highs = [], []

    def ends(rows):
        lows.append(rows[:1])
        highs.append(rows[rows.shape[0] - 1 :])

    boxes = {}
    for y in range(size_y):
        for z in range(size_z):
            rows = base[y, z]
            boxes[y, z] = lift(rows)
            ends(rows.astype(F32))

    def grouped(boxes, y, z, rows):
        pieces = []
        for u in range(2):
            for v in range(2):
                for w in range(2):
                    pieces.append(boxes[2 * y + v, 2 * z + w][u * rows : (u + 1) * rows])
        return jnp.concatenate(pieces, axis=1)

    coarse = {}
    for y in range(size_y // 2):
        for z in range(size_z // 2):
            group = grouped(boxes, y, z, half)
            ends(group)
            middle[y, z] = group.astype(BF)
            coarse[y, z] = lift(group.astype(BF))
    for y in range(size_y // 4):
        for z in range(size_z // 4):
            group = grouped(coarse, y, z, part)
            ends(group)
            top[y, z] = jnp.concatenate([group, jnp.zeros_like(group)], axis=0).astype(BF)
    fill = [jnp.zeros((-len(lows) % 16, width), F32)]
    low[...] = jnp.concatenate(lows + fill, axis=0).astype(BF)
    high[...] = jnp.concatenate(highs + fill, axis=0).astype(BF)


def lifted(base, weights):
    size_y, size_z, size_x, width = base.shape
    count = size_y * size_z + (size_y // 2) * (size_z // 2) + (size_y // 4) * (size_z // 4)
    ends = jax.ShapeDtypeStruct((-(-count // 16) * 16, width), BF)
    return pl.pallas_call(
        lift_kernel,
        out_shape=(
            jax.ShapeDtypeStruct((size_y // 2, size_z // 2, size_x // 2, width), BF),
            jax.ShapeDtypeStruct((size_y // 4, size_z // 4, size_x // 2, width), BF),
            ends,
            ends,
        ),
        in_specs=[WHOLE] * 2,
        out_specs=(WHOLE,) * 4,
        compiler_params=params(24),
        name="lift",
    )(base, weights)


def turn_operators(weight, blocks, source, at):
    coeffs, _, count = weight.shape
    lanes = blocks.shape[1]
    part = widened(weight[source, :, at : min(at + lanes, count)].astype(F32))
    blocks[pl.ds(at * coeffs + source, lanes, stride=coeffs), :] = widened(part.T)


def number_of(first, second, third):
    number = 0
    for i in range(first * 49 + second * 7 + third):
        number += not all(2 <= j <= 4 for j in (i // 49, i // 7 % 7, i % 7))
    return number


def fill_entry(blocks, table, first, second, third, coeffs):
    def found(at):
        spot = (first, second, at)
        if all(2 <= i <= 4 for i in spot):
            return jnp.zeros((coeffs, blocks.shape[1]), F32)
        before = number_of(*spot)
        return blocks[before * coeffs : (before + 1) * coeffs]

    rows = []
    for s in range(2):
        at = 2 * third + s
        rows.append(found(at + 1) + pltpu.roll(found(at), coeffs, 1))
    rows = jnp.concatenate(rows, axis=0)
    table[third, first, second] = rows[:, : 2 * coeffs].astype(BF)


SLOTS = 8
SHIFTS = [
    (dx, dy, dz)
    for dx in range(3)
    for dy in (1, 0, 2)
    for dz in (1, 0, 2)
    if (dx, dy, dz) != (1, 1, 1)
]


def moved_rows(rows, low, high):
    part = 8
    q = [rows[i : i + part] for i in range(0, rows.shape[0], part)]
    count = len(q)
    before = jnp.concatenate([low, q[-1][:-1]], axis=0)
    after = jnp.concatenate([q[0][1:], high], axis=0)
    if count == 4:
        return [before, q[2], q[0], q[1]], [q[2], q[3], q[1], after]
    if count == 2:
        return [before, q[0]], [q[1], after]
    return [before], [after]


def widened(rows):
    fill = -rows.shape[1] % 128
    if fill:
        zeros = jnp.zeros((rows.shape[0], fill), rows.dtype)
        rows = jnp.concatenate([rows, zeros], axis=1)
    return rows


def store_moved(rows, low, high, copies, y, z, fill=False, wanted=range(3)):
    rows = widened(rows.astype(F32))
    one, two = moved_rows(rows, widened(low), widened(high))
    three = [one, [rows], two]
    for dx in wanted:
        if fill:
            three[dx] = three[dx] + [jnp.zeros_like(rows)]
        copies[dx, y, z] = jnp.concatenate(three[dx], axis=0).astype(BF)


def operator(table, shift, kernels, slot):
    dx, dy, dz = shift
    slot = slot % kernels.shape[0]
    pair = table.shape[4]
    for sx in range(2):
        for sy in range(2):
            parts = [
                table[dz, 2 * dx + sx - tx + 1, 2 * dy + sy - ty + 1]
                for tx in range(2)
                for ty in range(2)
            ]
            at = (2 * sx + sy) * pair
            kernels[slot, at : at + pair] = widened(jnp.concatenate(parts, axis=1))
    rows = kernels.shape[1]
    if rows > 4 * pair:
        kernels[slot, 4 * pair :] = jnp.zeros((rows - 4 * pair, kernels.shape[2]), BF)
    return kernels[slot]


def first_kernel(weight, leaf, below, above, _, table, total, blocks, leaves, kernels):
    coeffs, _, offsets = weight.shape
    size_y, size_z, size_x, width = leaf.shape
    lanes = blocks.shape[1]

    low = below[: size_y * size_z].astype(F32)
    high = above[: size_y * size_z].astype(F32)

    def move(dx):
        steps = []
        for y in range(size_y):
            for z in range(size_z):
                ends = [rows[y * size_z + z : y * size_z + z + 1] for rows in (low, high)]
                steps.append(
                    functools.partial(
                        store_moved, leaf[y, z], *ends, leaves, y, z, wanted=(dx,)
                    )
                )
        return steps

    for step in move(0):
        step()

    def turn(source, carry):
        turn_operators(weight, blocks, source, 0)
        return carry

    lax.fori_loop(0, coeffs, turn, 0, unroll=8)

    tasks = []

    def due(steps, begin, end):
        for i, step in enumerate(steps):
            tasks.append((begin + i * (end - begin) // len(steps), step))

    def needs(shift):
        dx, dy, dz = shift
        return number_of(2 * dx + 2, 2 * dy + 2, 2 * dz + 2)

    begin = 0
    for at in range(lanes, offsets, lanes):
        end = min(slot for slot, shift in enumerate(SHIFTS) if needs(shift) >= at)
        begin = min(begin, end - 1)
        steps = [
            functools.partial(turn_operators, weight, blocks, source, at)
            for source in range(coeffs)
        ]
        due(steps, begin, end)
        begin = end
    for dx in range(1, 3):
        end = min(slot for slot, shift in enumerate(SHIFTS) if shift[0] == dx)
        due(move(dx), end - 8, end)

    done = set()

    def prepare(dx, dy, dz):
        for first in range(2 * dx, 2 * dx + 3):
            for second in range(2 * dy, 2 * dy + 3):
                if (dz, first, second) not in done:
                    done.add((dz, first, second))
                    fill_entry(blocks, table, first, second, dz, coeffs)

    for slot, (dx, dy, dz) in enumerate(SHIFTS):
        prepare(dx, dy, dz)
        kernel = operator(table, (dx, dy, dz), kernels, slot)
        first_z, last_z = max(0, 1 - dz), size_z - max(0, dz - 1)
        first_y, last_y = max(0, 1 - dy), size_y - max(0, dy - 1)
        count = (last_z - first_z) * size_x
        rows = leaves[
            dx, first_y + dy - 1 : last_y + dy - 1, first_z + dz - 1 : last_z + dz - 1
        ].reshape(-1, leaves.shape[4])
        product = jnp.dot(rows, kernel, preferred_element_type=F32)
        for i in range(last_y - first_y):
            at = ((first_y + i) * size_z + first_z) * size_x
            piece = product[i * count : (i + 1) * count]
            total[at : at + count] = piece if slot == 0 else total[at : at + count] + piece
        for when, step in tasks:
            if when == slot:
                step()
    for dx, dy, dz in [(dx, dy, dz) for dx in range(3) for dy in range(3) for dz in range(3)]:
        prepare(dx, dy, dz)


def first_part(transfer_weight, leaf, below, above, after):
    count, coeffs, _ = transfer_weight.shape
    size_y, size_z, size_x, width = leaf.shape
    wide = -(-width // 128) * 128
    return pl.pallas_call(
        first_kernel,
        out_shape=(
            jax.ShapeDtypeStruct((3, 7, 7, 2 * coeffs, 2 * coeffs), BF),
            jax.ShapeDtypeStruct((size_y * size_z * size_x, wide), F32),
        ),
        in_specs=[WHOLE] * 4 + [ANYWHERE],
        out_specs=(WHOLE, WHOLE),
        scratch_shapes=[
            pltpu.VMEM((-(-count // 128) * 128 * coeffs, 128), F32),
            pltpu.VMEM((3, size_y, size_z, size_x, wide), BF),
            pltpu.VMEM((SLOTS, wide, wide), BF),
        ],
        compiler_params=params(32),
        cost_estimate=pl.CostEstimate(flops=2 * 10**10, bytes_accessed=10**7, transcendentals=0),
        name="first",
    )(transfer_weight.transpose(1, 2, 0), leaf, below, above, after)


def far_kernel(
    odd, near, table, middle, top, below_x, above_x, got_z, got_y, got_yz, down, out,
    total, leaves, middles, tops, kernels, upper, out_rows, sent,
):
    size_y, size_z = 2 * middle.shape[0], 2 * middle.shape[1]
    half, width = middle.shape[2:]
    size_x = 2 * half
    coeffs = width // 8
    none = jnp.zeros((1, width), F32)
    odd_y, odd_z = odd[0] == 1, odd[1] == 1

    def chosen(is_odd, side, got, rows):
        first, other = got[0, rows], got[1, rows]
        pair = (first, other) if side == 0 else (other, first)
        return jnp.where(is_odd, pair[0], pair[1])

    def corner(side_y, side_z, rows):
        near_y = [chosen(odd_z, side_z, got_yz.at[i], rows) for i in range(2)]
        pair = near_y if side_y == 0 else near_y[::-1]
        return jnp.where(odd_y, pair[0], pair[1])

    sizes = [(size_y, size_z, size_x), (size_y // 2, size_z // 2, half), (size_y // 4, size_z // 4, half)]
    own = (None, middle, top)
    slabs = [{}, {}, {}]
    at_x = 0
    sides_x = [below_x[...].astype(F32), above_x[...].astype(F32)]
    for level, (count_y, count_z, rows) in enumerate(sizes):
        for y in range(count_y):
            for z in range(count_z):
                if level > 0:
                    ends = [side[at_x : at_x + 1] for side in sides_x]
                    slabs[level][y + 1, z + 1] = [own[level][y, z], *ends]
                at_x += 1

    def unpack(read, spots):
        at = 0
        for level, (_, _, rows) in enumerate(sizes):
            for spot in spots(level):
                slabs[level][spot] = [read(slice(at, at + rows))]
                at += rows
        count = 2 * sum(len(spots(level)) for level in range(3))
        tail = read(slice(at, at + -(-count // 16) * 16)).astype(F32)
        at = 0
        for level in range(3):
            for end in range(2):
                for spot in spots(level):
                    slabs[level][spot].append(tail[at : at + 1])
                    at += 1

    for side in range(2):
        unpack(
            functools.partial(chosen, odd_z, side, got_z),
            lambda level: [(y + 1, side * (sizes[level][1] + 1)) for y in range(sizes[level][0])],
        )
        unpack(
            functools.partial(chosen, odd_y, side, got_y),
            lambda level: [(side * (sizes[level][0] + 1), z + 1) for z in range(sizes[level][1])],
        )
        for other in range(2):
            unpack(
                functools.partial(corner, side, other),
                lambda level: [(side * (sizes[level][0] + 1), other * (sizes[level][1] + 1))],
            )

    copies = (leaves, middles, tops)

    def move(level, wanted):
        steps = []
        for (y, z), (rows, low, high) in slabs[level].items():
            if level == 2:
                rows = rows[: half // 2]
            steps.append(
                functools.partial(
                    store_moved, rows, low, high, copies[level], y, z, level == 2, wanted
                )
            )
        return steps

    for step in move(1, (0,)) + move(2, (0,)):
        step()
    tasks = []

    def due(steps, begin, end):
        for i, step in enumerate(steps):
            tasks.append((begin + i * (end - begin) // len(steps), step))

    for dx in range(1, 3):
        end = min(slot for slot, shift in enumerate(SHIFTS) if shift[0] == dx)
        due(move(1, (dx,)) + move(2, (dx,)), end - 8, end)
    due(move(0, range(3)), 0, len(SHIFTS))

    leaf_rows = size_y * size_z * size_x
    wide = kernels.shape[1]
    made = []
    for slot, (dx, dy, dz) in enumerate(SHIFTS):
        made.append(operator(table, (dx, dy, dz), kernels, slot))
        rows = [
            middles[dx, dy : dy + size_y // 2, dz : dz + size_z // 2].reshape(-1, wide),
            tops[dx, dy : dy + size_y // 4, dz : dz + size_z // 4].reshape(-1, wide),
        ]
        rows = jnp.concatenate(rows, axis=0)
        product = jnp.dot(rows, made[slot], preferred_element_type=F32)[:, :width]
        upper[...] = product if slot == 0 else upper[...] + product
        for when, step in tasks:
            if when == slot:
                step()

    weight = down[down.shape[0] // 2 :][:coeffs]

    def spread(count_y, count_z, parent, rows):
        pieces = []
        for y in range(2 * count_y):
            for z in range(2 * count_z):
                for u in range(2):
                    octant = 4 * u + 2 * (y % 2) + z % 2
                    values = parent(y // 2, z // 2)
                    pieces.append(values[:rows, octant * coeffs : (octant + 1) * coeffs])
        return jnp.concatenate(pieces, axis=0).astype(BF)

    middle_rows = leaf_rows // 8

    def top_of(y, z):
        at = middle_rows + (y * (size_z // 4) + z) * half
        return upper[at : at + half]

    boxes = spread(size_y // 4, size_z // 4, top_of, half // 2)
    local = upper[:middle_rows] + jnp.dot(boxes, weight, preferred_element_type=F32)

    def middle_of(y, z):
        at = (y * (size_z // 2) + z) * half
        return local[at : at + half]

    boxes = spread(size_y // 2, size_z // 2, middle_of, half)
    part_x = half // 2
    step = size_z * size_x
    touched = set()

    def finish(y):
        part = slice(y * step, (y + 1) * step)
        product = []

        def add(z):
            if not product:
                product.append(jnp.dot(boxes[part], weight, preferred_element_type=F32))
            at = z * size_x
            here = slice(y * step + at, y * step + at + size_x)
            source = total if here.start in touched else near
            rows = source[here] + widened(product[0][at : at + size_x])
            for i in range(size_x):
                a, b, x = i // half, i // part_x % 2, i % part_x
                out_rows[4 * x + 2 * b + a, y, z : z + 1] = rows[i : i + 1, :width]

        return [functools.partial(add, z) for z in range(size_z)]

    leaving = []

    def leave(ys):
        rows = pl.ds(ys.start, len(ys))
        copy = pltpu.make_async_copy(out_rows.at[:, rows], out.at[:, rows], sent.at[len(leaving)])
        copy.start()
        leaving.append(copy)

    steps = []
    halves = [range(0, size_y // 2), range(size_y // 2, size_y)]
    for ys in halves:
        count = -(-len(steps) // (len(SHIFTS) - 2))
        for slot, (dx, dy, dz) in enumerate(SHIFTS):
            places, rows = [], []
            for y in ys:
                for z in range(size_z):
                    if y + dy in (0, size_y + 1) or z + dz in (0, size_z + 1):
                        places.append((y * size_z + z) * size_x)
                        rows.append(leaves[dx, y + dy, z + dz])
            if rows:
                rows = jnp.concatenate(rows, axis=0)
                product = jnp.dot(rows, kernels[slot], preferred_element_type=F32)
                for i, at in enumerate(places):
                    source = total if at in touched else near
                    touched.add(at)
                    total[at : at + size_x] = (
                        source[at : at + size_x] + product[i * size_x : (i + 1) * size_x]
                    )
            for one in steps[:count]:
                one()
            steps = steps[count:]
        assert not steps
        if ys is not halves[0]:
            leave(halves[0])
        steps = [one for y in ys for one in finish(y)]
    for one in steps:
        one()
    leave(halves[1])
    for copy in leaving:
        copy.wait()


def far(odd, near, table, middle, top, halos, down):
    rows, wide = near.shape
    width = middle.shape[3]
    size_y, size_z, half = 2 * middle.shape[0], 2 * middle.shape[1], middle.shape[2]
    upper = half * ((size_y // 2) * (size_z // 2) + (size_y // 4) * (size_z // 4))
    return pl.pallas_call(
        far_kernel,
        out_shape=jax.ShapeDtypeStruct((2 * half, size_y, size_z, width), F32),
        in_specs=[pl.BlockSpec(memory_space=pltpu.SMEM)] + [WHOLE] * 10,
        out_specs=HBM,
        scratch_shapes=[
            pltpu.VMEM((rows, wide), F32),
            pltpu.VMEM((3, size_y + 2, size_z + 2, 2 * half, wide), BF),
            pltpu.VMEM((3, size_y // 2 + 2, size_z // 2 + 2, half, wide), BF),
            pltpu.VMEM((3, size_y // 4 + 2, size_z // 4 + 2, half, wide), BF),
            pltpu.VMEM((len(SHIFTS), wide, wide), BF),
            pltpu.VMEM((upper, width), F32),
            pltpu.VMEM((2 * half, size_y, size_z, width), F32),
            pltpu.SemaphoreType.DMA((2,)),
        ],
        compiler_params=params(42),
        name="far",
    )(odd, near, table, middle, top, *halos, down)


def shards(densities, upward_weight, transfer_weight, downward_weight):
    size_x, size_y, size_z, width = densities.shape
    fill = ((0, -downward_weight.shape[0] % 16), (0, 0))
    weights = [jnp.pad(upward_weight.T, fill), jnp.pad(downward_weight, fill)]
    weights = jnp.concatenate(weights, axis=0)
    base = densities.reshape(size_x // 4, 2, 2, size_y, size_z, width)
    base = base.transpose(3, 4, 2, 1, 0, 5).reshape(size_y, size_z, size_x, width)
    middle, top, low, high = lifted(base, weights)
    levels = [base, middle, top]

    def packed(pieces):
        rows = jnp.concatenate([piece.reshape(-1, width) for piece in pieces], axis=0)
        return jnp.pad(rows, ((0, -rows.shape[0] % 16), (0, 0)))

    def unpacked(flat, shapes):
        pieces, at = [], 0
        for shape in shapes:
            count = 1
            for extent in shape:
                count *= extent
            pieces.append(flat[at : at + count].reshape(shape + (width,)))
            at += count
        return pieces

    first, other = exchange(low, high, "gx")
    odd = is_odd("gx")
    below_x, above_x = jnp.where(odd, first, other), jnp.where(odd, other, first)
    shapes = [level.shape[:2] for level in levels]
    sides = [
        jnp.stack(both) for both in zip(unpacked(below_x, shapes), unpacked(above_x, shapes))
    ]

    def face_z(at):
        return packed([level[:, at] for level in levels] + [side[:, :, at] for side in sides])

    def face_y(at):
        return packed([level[at] for level in levels] + [side[:, at] for side in sides])

    def corner(at_y, at_z):
        rows = [level[at_y, at_z] for level in levels] + [side[:, at_y, at_z] for side in sides]
        return packed(rows)

    low_z = face_z(0)
    got_z = jnp.stack(exchange(low_z, face_z(-1), "gz"))
    got_y = jnp.stack(exchange(face_y(0), face_y(-1), "gy"))
    got_yz = exchange_corners([[corner(y, z) for z in (0, -1)] for y in (0, -1)], "gy", "gz")
    table, near = first_part(transfer_weight, base, below_x, above_x, low_z)
    odd = jnp.stack([is_odd("gy"), is_odd("gz")]).astype(jnp.int32)
    halos = (below_x, above_x, got_z, got_y, got_yz)
    return far(odd, near, table, middle, top, halos, weights)


def solution(mesh):
    placed = (P("gx", "gy", "gz", None), P(), P(), P())
    return jax.shard_map(
        shards, mesh=mesh, in_specs=placed, out_specs=P("gx", "gy", "gz", None), check_vma=False
    )
```

```python
import functools

import jax
import jax.numpy as jnp
from jax import lax
from jax.experimental import pallas as pl
from jax.experimental.pallas import tpu as pltpu
from jax.sharding import PartitionSpec as P

BF = jnp.bfloat16
F32 = jnp.float32
ANYWHERE = pl.BlockSpec(memory_space=pl.ANY)
HBM = pl.BlockSpec(memory_space=pltpu.HBM)
WHOLE = pl.BlockSpec(memory_space=pltpu.VMEM)


def params(mib):
    return pltpu.CompilerParams(vmem_limit_bytes=mib * 2**20)


def rounds(axis):
    count = lax.axis_size(axis)
    return [[(i, i + 1) for i in range(first, count - 1, 2)] for first in (0, 1)]


def swapped(block, axis, pairs):
    both = pairs + [(two, one) for one, two in pairs]
    return lax.ppermute(block, axis, both) if pairs else jnp.zeros_like(block)


def is_odd(axis):
    return lax.axis_index(axis) % 2 == 1


def exchange(low, high, axis):
    odd = is_odd(axis)
    first, other = rounds(axis)
    got = swapped(jnp.where(odd, low, high), axis, first)
    return got, swapped(jnp.where(odd, high, low), axis, other)


def exchange_corners(faces, axis_y, axis_z):
    odd_y, odd_z = is_odd(axis_y), is_odd(axis_z)
    count_z = lax.axis_size(axis_z)
    result = []
    for round_y, pairs_y in enumerate(rounds(axis_y)):
        low_y, high_y = faces if round_y == 0 else faces[::-1]
        for round_z, pairs_z in enumerate(rounds(axis_z)):
            low = [jnp.where(odd_y, one, two) for one, two in zip(low_y, high_y)]
            low = low if round_z == 0 else low[::-1]
            pairs = []
            for one, two in pairs_y:
                for three, four in pairs_z:
                    pairs.append((one * count_z + three, two * count_z + four))
                    pairs.append((one * count_z + four, two * count_z + three))
            face = jnp.where(odd_z, low[0], low[1])
            result.append(swapped(face, (axis_y, axis_z), pairs))
    return jnp.stack(result).reshape(2, 2, *result[0].shape)


def lift_kernel(base, weight, middle, top, low, high):
    size_y, size_z, size_x, width = base.shape
    half, part = size_x // 2, size_x // 4
    up = weight[: weight.shape[0] // 2][: width // 8]

    def lift(rows):
        product = lax.dot_general(rows, up, (((1,), (1,)), ((), ())), preferred_element_type=F32)
        return product.astype(BF).astype(F32)

    lows, highs = [], []

    def ends(rows):
        lows.append(rows[:1])
        highs.append(rows[rows.shape[0] - 1 :])

    boxes = {}
    for y in range(size_y):
        for z in range(size_z):
            rows = base[y, z]
            boxes[y, z] = lift(rows)
            ends(rows.astype(F32))

    def grouped(boxes, y, z, rows):
        pieces = []
        for u in range(2):
            for v in range(2):
                for w in range(2):
                    pieces.append(boxes[2 * y + v, 2 * z + w][u * rows : (u + 1) * rows])
        return jnp.concatenate(pieces, axis=1)

    coarse = {}
    for y in range(size_y // 2):
        for z in range(size_z // 2):
            group = grouped(boxes, y, z, half)
            ends(group)
            middle[y, z] = group.astype(BF)
            coarse[y, z] = lift(group.astype(BF))
    for y in range(size_y // 4):
        for z in range(size_z // 4):
            group = grouped(coarse, y, z, part)
            ends(group)
            top[y, z] = jnp.concatenate([group, jnp.zeros_like(group)], axis=0).astype(BF)
    fill = [jnp.zeros((-len(lows) % 16, width), F32)]
    low[...] = jnp.concatenate(lows + fill, axis=0).astype(BF)
    high[...] = jnp.concatenate(highs + fill, axis=0).astype(BF)


def lifted(base, weights):
    size_y, size_z, size_x, width = base.shape
    count = size_y * size_z + (size_y // 2) * (size_z // 2) + (size_y // 4) * (size_z // 4)
    ends = jax.ShapeDtypeStruct((-(-count // 16) * 16, width), BF)
    return pl.pallas_call(
        lift_kernel,
        out_shape=(
            jax.ShapeDtypeStruct((size_y // 2, size_z // 2, size_x // 2, width), BF),
            jax.ShapeDtypeStruct((size_y // 4, size_z // 4, size_x // 2, width), BF),
            ends,
            ends,
        ),
        in_specs=[WHOLE] * 2,
        out_specs=(WHOLE,) * 4,
        compiler_params=params(24),
        name="lift",
    )(base, weights)


def turn_operators(weight, blocks, source, at):
    coeffs, _, count = weight.shape
    lanes = blocks.shape[1]
    part = widened(weight[source, :, at : min(at + lanes, count)].astype(F32))
    blocks[pl.ds(at * coeffs + source, lanes, stride=coeffs), :] = widened(part.T)


def number_of(first, second, third):
    number = 0
    for i in range(first * 49 + second * 7 + third):
        number += not all(2 <= j <= 4 for j in (i // 49, i // 7 % 7, i % 7))
    return number


def fill_entry(blocks, table, first, second, third, coeffs):
    def found(at):
        spot = (first, second, at)
        if all(2 <= i <= 4 for i in spot):
            return jnp.zeros((coeffs, blocks.shape[1]), F32)
        before = number_of(*spot)
        return blocks[before * coeffs : (before + 1) * coeffs]

    rows = []
    for s in range(2):
        at = 2 * third + s
        rows.append(found(at + 1) + pltpu.roll(found(at), coeffs, 1))
    rows = jnp.concatenate(rows, axis=0)
    table[third, first, second] = rows[:, : 2 * coeffs].astype(BF)


SLOTS = 8
SHIFTS = [
    (dx, dy, dz)
    for dx in range(3)
    for dy in (1, 0, 2)
    for dz in (1, 0, 2)
    if (dx, dy, dz) != (1, 1, 1)
]


def moved_rows(rows, low, high):
    part = 8
    q = [rows[i : i + part] for i in range(0, rows.shape[0], part)]
    count = len(q)
    before = jnp.concatenate([low, q[-1][:-1]], axis=0)
    after = jnp.concatenate([q[0][1:], high], axis=0)
    if count == 4:
        return [before, q[2], q[0], q[1]], [q[2], q[3], q[1], after]
    if count == 2:
        return [before, q[0]], [q[1], after]
    return [before], [after]


def widened(rows):
    fill = -rows.shape[1] % 128
    if fill:
        zeros = jnp.zeros((rows.shape[0], fill), rows.dtype)
        rows = jnp.concatenate([rows, zeros], axis=1)
    return rows


def store_moved(rows, low, high, copies, y, z, fill=False, wanted=range(3)):
    rows = widened(rows.astype(F32))
    one, two = moved_rows(rows, widened(low), widened(high))
    three = [one, [rows], two]
    for dx in wanted:
        if fill:
            three[dx] = three[dx] + [jnp.zeros_like(rows)]
        copies[dx, y, z] = jnp.concatenate(three[dx], axis=0).astype(BF)


def operator(table, shift, kernels, slot):
    dx, dy, dz = shift
    slot = slot % kernels.shape[0]
    pair = table.shape[4]
    for sx in range(2):
        for sy in range(2):
            parts = [
                table[dz, 2 * dx + sx - tx + 1, 2 * dy + sy - ty + 1]
                for tx in range(2)
                for ty in range(2)
            ]
            at = (2 * sx + sy) * pair
            kernels[slot, at : at + pair] = widened(jnp.concatenate(parts, axis=1))
    rows = kernels.shape[1]
    if rows > 4 * pair:
        kernels[slot, 4 * pair :] = jnp.zeros((rows - 4 * pair, kernels.shape[2]), BF)
    return kernels[slot]


def first_kernel(weight, leaf, below, above, _, table, total, blocks, leaves, kernels):
    coeffs, _, offsets = weight.shape
    size_y, size_z, size_x, width = leaf.shape
    lanes = blocks.shape[1]

    low = below[: size_y * size_z].astype(F32)
    high = above[: size_y * size_z].astype(F32)

    def move(dx):
        steps = []
        for y in range(size_y):
            for z in range(size_z):
                ends = [rows[y * size_z + z : y * size_z + z + 1] for rows in (low, high)]
                steps.append(
                    functools.partial(
                        store_moved, leaf[y, z], *ends, leaves, y, z, wanted=(dx,)
                    )
                )
        return steps

    for step in move(0):
        step()

    def turn(source, carry):
        turn_operators(weight, blocks, source, 0)
        return carry

    lax.fori_loop(0, coeffs, turn, 0, unroll=28)

    tasks = []

    def due(steps, begin, end):
        for i, step in enumerate(steps):
            tasks.append((begin + i * (end - begin) // len(steps), step))

    def needs(shift):
        dx, dy, dz = shift
        return number_of(2 * dx + 2, 2 * dy + 2, 2 * dz + 2)

    begin = 0
    for at in range(lanes, offsets, lanes):
        end = min(slot for slot, shift in enumerate(SHIFTS) if needs(shift) >= at)
        begin = min(begin, end - 1)
        steps = [
            functools.partial(turn_operators, weight, blocks, source, at)
            for source in range(coeffs)
        ]
        due(steps, begin, end)
        begin = end
    for dx in range(1, 3):
        end = min(slot for slot, shift in enumerate(SHIFTS) if shift[0] == dx)
        due(move(dx), end - 8, end)

    done = set()

    def prepare(dx, dy, dz):
        for first in range(2 * dx, 2 * dx + 3):
            for second in range(2 * dy, 2 * dy + 3):
                if (dz, first, second) not in done:
                    done.add((dz, first, second))
                    fill_entry(blocks, table, first, second, dz, coeffs)

    for slot, (dx, dy, dz) in enumerate(SHIFTS):
        prepare(dx, dy, dz)
        kernel = operator(table, (dx, dy, dz), kernels, slot)
        first_z, last_z = max(0, 1 - dz), size_z - max(0, dz - 1)
        first_y, last_y = max(0, 1 - dy), size_y - max(0, dy - 1)
        count = (last_z - first_z) * size_x
        rows = leaves[
            dx, first_y + dy - 1 : last_y + dy - 1, first_z + dz - 1 : last_z + dz - 1
        ].reshape(-1, leaves.shape[4])
        product = jnp.dot(rows, kernel, preferred_element_type=F32)
        for i in range(last_y - first_y):
            at = ((first_y + i) * size_z + first_z) * size_x
            piece = product[i * count : (i + 1) * count]
            total[at : at + count] = piece if slot == 0 else total[at : at + count] + piece
        for when, step in tasks:
            if when == slot:
                step()
    for dx, dy, dz in [(dx, dy, dz) for dx in range(3) for dy in range(3) for dz in range(3)]:
        prepare(dx, dy, dz)


def first_part(transfer_weight, leaf, below, above, after):
    count, coeffs, _ = transfer_weight.shape
    size_y, size_z, size_x, width = leaf.shape
    wide = -(-width // 128) * 128
    return pl.pallas_call(
        first_kernel,
        out_shape=(
            jax.ShapeDtypeStruct((3, 7, 7, 2 * coeffs, 2 * coeffs), BF),
            jax.ShapeDtypeStruct((size_y * size_z * size_x, wide), F32),
        ),
        in_specs=[WHOLE] * 4 + [ANYWHERE],
        out_specs=(WHOLE, WHOLE),
        scratch_shapes=[
            pltpu.VMEM((-(-count // 128) * 128 * coeffs, 128), F32),
            pltpu.VMEM((3, size_y, size_z, size_x, wide), BF),
            pltpu.VMEM((SLOTS, wide, wide), BF),
        ],
        compiler_params=params(32),
        cost_estimate=pl.CostEstimate(flops=2 * 10**10, bytes_accessed=10**7, transcendentals=0),
        name="first",
    )(transfer_weight.transpose(1, 2, 0), leaf, below, above, after)


def far_kernel(
    odd, near, table, middle, top, below_x, above_x, got_z, got_y, got_yz, down, out,
    total, leaves, middles, tops, kernels, upper, out_rows, sent,
):
    size_y, size_z = 2 * middle.shape[0], 2 * middle.shape[1]
    half, width = middle.shape[2:]
    size_x = 2 * half
    coeffs = width // 8
    none = jnp.zeros((1, width), F32)
    odd_y, odd_z = odd[0] == 1, odd[1] == 1

    def chosen(is_odd, side, got, rows):
        first, other = got[0, rows], got[1, rows]
        pair = (first, other) if side == 0 else (other, first)
        return jnp.where(is_odd, pair[0], pair[1])

    def corner(side_y, side_z, rows):
        near_y = [chosen(odd_z, side_z, got_yz.at[i], rows) for i in range(2)]
        pair = near_y if side_y == 0 else near_y[::-1]
        return jnp.where(odd_y, pair[0], pair[1])

    sizes = [(size_y, size_z, size_x), (size_y // 2, size_z // 2, half), (size_y // 4, size_z // 4, half)]
    own = (None, middle, top)
    slabs = [{}, {}, {}]
    at_x = 0
    sides_x = [below_x[...].astype(F32), above_x[...].astype(F32)]
    for level, (count_y, count_z, rows) in enumerate(sizes):
        for y in range(count_y):
            for z in range(count_z):
                if level > 0:
                    ends = [side[at_x : at_x + 1] for side in sides_x]
                    slabs[level][y + 1, z + 1] = [own[level][y, z], *ends]
                at_x += 1

    def unpack(read, spots):
        at = 0
        for level, (_, _, rows) in enumerate(sizes):
            for spot in spots(level):
                slabs[level][spot] = [read(slice(at, at + rows))]
                at += rows
        count = 2 * sum(len(spots(level)) for level in range(3))
        tail = read(slice(at, at + -(-count // 16) * 16)).astype(F32)
        at = 0
        for level in range(3):
            for end in range(2):
                for spot in spots(level):
                    slabs[level][spot].append(tail[at : at + 1])
                    at += 1

    for side in range(2):
        unpack(
            functools.partial(chosen, odd_z, side, got_z),
            lambda level: [(y + 1, side * (sizes[level][1] + 1)) for y in range(sizes[level][0])],
        )
        unpack(
            functools.partial(chosen, odd_y, side, got_y),
            lambda level: [(side * (sizes[level][0] + 1), z + 1) for z in range(sizes[level][1])],
        )
        for other in range(2):
            unpack(
                functools.partial(corner, side, other),
                lambda level: [(side * (sizes[level][0] + 1), other * (sizes[level][1] + 1))],
            )

    copies = (leaves, middles, tops)

    def move(level, wanted):
        steps = []
        for (y, z), (rows, low, high) in slabs[level].items():
            if level == 2:
                rows = rows[: half // 2]
            steps.append(
                functools.partial(
                    store_moved, rows, low, high, copies[level], y, z, level == 2, wanted
                )
            )
        return steps

    for step in move(1, (0,)) + move(2, (0,)):
        step()
    tasks = []

    def due(steps, begin, end):
        for i, step in enumerate(steps):
            tasks.append((begin + i * (end - begin) // len(steps), step))

    for dx in range(1, 3):
        end = min(slot for slot, shift in enumerate(SHIFTS) if shift[0] == dx)
        due(move(1, (dx,)) + move(2, (dx,)), end - 8, end)
    due(move(0, range(3)), 0, len(SHIFTS))

    leaf_rows = size_y * size_z * size_x
    wide = kernels.shape[1]
    made = []
    for slot, (dx, dy, dz) in enumerate(SHIFTS):
        made.append(operator(table, (dx, dy, dz), kernels, slot))
        rows = [
            middles[dx, dy : dy + size_y // 2, dz : dz + size_z // 2].reshape(-1, wide),
            tops[dx, dy : dy + size_y // 4, dz : dz + size_z // 4].reshape(-1, wide),
        ]
        rows = jnp.concatenate(rows, axis=0)
        product = jnp.dot(rows, made[slot], preferred_element_type=F32)[:, :width]
        upper[...] = product if slot == 0 else upper[...] + product
        for when, step in tasks:
            if when == slot:
                step()

    weight = down[down.shape[0] // 2 :][:coeffs]

    def spread(count_y, count_z, parent, rows):
        pieces = []
        for y in range(2 * count_y):
            for z in range(2 * count_z):
                for u in range(2):
                    octant = 4 * u + 2 * (y % 2) + z % 2
                    values = parent(y // 2, z // 2)
                    pieces.append(values[:rows, octant * coeffs : (octant + 1) * coeffs])
        return jnp.concatenate(pieces, axis=0).astype(BF)

    middle_rows = leaf_rows // 8

    def top_of(y, z):
        at = middle_rows + (y * (size_z // 4) + z) * half
        return upper[at : at + half]

    boxes = spread(size_y // 4, size_z // 4, top_of, half // 2)
    local = upper[:middle_rows] + jnp.dot(boxes, weight, preferred_element_type=F32)

    def middle_of(y, z):
        at = (y * (size_z // 2) + z) * half
        return local[at : at + half]

    boxes = spread(size_y // 2, size_z // 2, middle_of, half)
    part_x = half // 2
    step = size_z * size_x
    touched = set()

    def finish(y):
        part = slice(y * step, (y + 1) * step)
        product = []

        def add(z):
            if not product:
                product.append(jnp.dot(boxes[part], weight, preferred_element_type=F32))
            at = z * size_x
            here = slice(y * step + at, y * step + at + size_x)
            source = total if here.start in touched else near
            rows = source[here] + widened(product[0][at : at + size_x])
            for i in range(size_x):
                a, b, x = i // half, i // part_x % 2, i % part_x
                out_rows[4 * x + 2 * b + a, y, z : z + 1] = rows[i : i + 1, :width]

        return [functools.partial(add, z) for z in range(size_z)]

    leaving = []

    def leave(ys):
        rows = pl.ds(ys.start, len(ys))
        copy = pltpu.make_async_copy(out_rows.at[:, rows], out.at[:, rows], sent.at[len(leaving)])
        copy.start()
        leaving.append(copy)

    steps = []
    halves = [range(0, size_y // 2), range(size_y // 2, size_y)]
    for ys in halves:
        count = -(-len(steps) // (len(SHIFTS) - 2))
        for slot, (dx, dy, dz) in enumerate(SHIFTS):
            places, rows = [], []
            for y in ys:
                for z in range(size_z):
                    if y + dy in (0, size_y + 1) or z + dz in (0, size_z + 1):
                        places.append((y * size_z + z) * size_x)
                        rows.append(leaves[dx, y + dy, z + dz])
            if rows:
                rows = jnp.concatenate(rows, axis=0)
                product = jnp.dot(rows, kernels[slot], preferred_element_type=F32)
                for i, at in enumerate(places):
                    source = total if at in touched else near
                    touched.add(at)
                    total[at : at + size_x] = (
                        source[at : at + size_x] + product[i * size_x : (i + 1) * size_x]
                    )
            for one in steps[:count]:
                one()
            steps = steps[count:]
        assert not steps
        if ys is not halves[0]:
            leave(halves[0])
        steps = [one for y in ys for one in finish(y)]
    for one in steps:
        one()
    leave(halves[1])
    for copy in leaving:
        copy.wait()


def far(odd, near, table, middle, top, halos, down):
    rows, wide = near.shape
    width = middle.shape[3]
    size_y, size_z, half = 2 * middle.shape[0], 2 * middle.shape[1], middle.shape[2]
    upper = half * ((size_y // 2) * (size_z // 2) + (size_y // 4) * (size_z // 4))
    return pl.pallas_call(
        far_kernel,
        out_shape=jax.ShapeDtypeStruct((2 * half, size_y, size_z, width), F32),
        in_specs=[pl.BlockSpec(memory_space=pltpu.SMEM)] + [WHOLE] * 10,
        out_specs=HBM,
        scratch_shapes=[
            pltpu.VMEM((rows, wide), F32),
            pltpu.VMEM((3, size_y + 2, size_z + 2, 2 * half, wide), BF),
            pltpu.VMEM((3, size_y // 2 + 2, size_z // 2 + 2, half, wide), BF),
            pltpu.VMEM((3, size_y // 4 + 2, size_z // 4 + 2, half, wide), BF),
            pltpu.VMEM((len(SHIFTS), wide, wide), BF),
            pltpu.VMEM((upper, width), F32),
            pltpu.VMEM((2 * half, size_y, size_z, width), F32),
            pltpu.SemaphoreType.DMA((2,)),
        ],
        compiler_params=params(42),
        name="far",
    )(odd, near, table, middle, top, *halos, down)


def shards(densities, upward_weight, transfer_weight, downward_weight):
    size_x, size_y, size_z, width = densities.shape
    fill = ((0, -downward_weight.shape[0] % 16), (0, 0))
    weights = [jnp.pad(upward_weight.T, fill), jnp.pad(downward_weight, fill)]
    weights = jnp.concatenate(weights, axis=0)
    base = densities.reshape(size_x // 4, 2, 2, size_y, size_z, width)
    base = base.transpose(3, 4, 2, 1, 0, 5).reshape(size_y, size_z, size_x, width)
    middle, top, low, high = lifted(base, weights)
    levels = [base, middle, top]

    def packed(pieces):
        rows = jnp.concatenate([piece.reshape(-1, width) for piece in pieces], axis=0)
        return jnp.pad(rows, ((0, -rows.shape[0] % 16), (0, 0)))

    def unpacked(flat, shapes):
        pieces, at = [], 0
        for shape in shapes:
            count = 1
            for extent in shape:
                count *= extent
            pieces.append(flat[at : at + count].reshape(shape + (width,)))
            at += count
        return pieces

    first, other = exchange(low, high, "gx")
    odd = is_odd("gx")
    below_x, above_x = jnp.where(odd, first, other), jnp.where(odd, other, first)
    shapes = [level.shape[:2] for level in levels]
    sides = [
        jnp.stack(both) for both in zip(unpacked(below_x, shapes), unpacked(above_x, shapes))
    ]

    def face_z(at):
        return packed([level[:, at] for level in levels] + [side[:, :, at] for side in sides])

    def face_y(at):
        return packed([level[at] for level in levels] + [side[:, at] for side in sides])

    def corner(at_y, at_z):
        rows = [level[at_y, at_z] for level in levels] + [side[:, at_y, at_z] for side in sides]
        return packed(rows)

    low_z = face_z(0)
    got_z = jnp.stack(exchange(low_z, face_z(-1), "gz"))
    got_y = jnp.stack(exchange(face_y(0), face_y(-1), "gy"))
    got_yz = exchange_corners([[corner(y, z) for z in (0, -1)] for y in (0, -1)], "gy", "gz")
    table, near = first_part(transfer_weight, base, below_x, above_x, low_z)
    odd = jnp.stack([is_odd("gy"), is_odd("gz")]).astype(jnp.int32)
    halos = (below_x, above_x, got_z, got_y, got_yz)
    return far(odd, near, table, middle, top, halos, weights)


def solution(mesh):
    placed = (P("gx", "gy", "gz", None), P(), P(), P())
    return jax.shard_map(
        shards, mesh=mesh, in_specs=placed, out_specs=P("gx", "gy", "gz", None), check_vma=False
    )
```

```python
import functools

import jax
import jax.numpy as jnp
from jax import lax
from jax.experimental import pallas as pl
from jax.experimental.pallas import tpu as pltpu
from jax.sharding import PartitionSpec as P

BF = jnp.bfloat16
F32 = jnp.float32
ANYWHERE = pl.BlockSpec(memory_space=pl.ANY)
HBM = pl.BlockSpec(memory_space=pltpu.HBM)
WHOLE = pl.BlockSpec(memory_space=pltpu.VMEM)


def params(mib):
    return pltpu.CompilerParams(vmem_limit_bytes=mib * 2**20)


def rounds(axis):
    count = lax.axis_size(axis)
    return [[(i, i + 1) for i in range(first, count - 1, 2)] for first in (0, 1)]


def swapped(block, axis, pairs):
    both = pairs + [(two, one) for one, two in pairs]
    return lax.ppermute(block, axis, both) if pairs else jnp.zeros_like(block)


def is_odd(axis):
    return lax.axis_index(axis) % 2 == 1


def exchange(low, high, axis):
    odd = is_odd(axis)
    first, other = rounds(axis)
    got = swapped(jnp.where(odd, low, high), axis, first)
    return got, swapped(jnp.where(odd, high, low), axis, other)


def exchange_corners(faces, axis_y, axis_z):
    odd_y, odd_z = is_odd(axis_y), is_odd(axis_z)
    count_z = lax.axis_size(axis_z)
    result = []
    for round_y, pairs_y in enumerate(rounds(axis_y)):
        low_y, high_y = faces if round_y == 0 else faces[::-1]
        for round_z, pairs_z in enumerate(rounds(axis_z)):
            low = [jnp.where(odd_y, one, two) for one, two in zip(low_y, high_y)]
            low = low if round_z == 0 else low[::-1]
            pairs = []
            for one, two in pairs_y:
                for three, four in pairs_z:
                    pairs.append((one * count_z + three, two * count_z + four))
                    pairs.append((one * count_z + four, two * count_z + three))
            face = jnp.where(odd_z, low[0], low[1])
            result.append(swapped(face, (axis_y, axis_z), pairs))
    return jnp.stack(result).reshape(2, 2, *result[0].shape)


def lift_kernel(base, weight, middle, top, low, high):
    size_y, size_z, size_x, width = base.shape
    half, part = size_x // 2, size_x // 4
    up = weight[: weight.shape[0] // 2][: width // 8]

    def lift(rows):
        product = lax.dot_general(rows, up, (((1,), (1,)), ((), ())), preferred_element_type=F32)
        return product.astype(BF).astype(F32)

    lows, highs = [], []

    def ends(rows):
        lows.append(rows[:1])
        highs.append(rows[rows.shape[0] - 1 :])

    boxes = {}
    lifted_rows = lift(base[...].reshape(-1, width))
    for y in range(size_y):
        for z in range(size_z):
            at = (y * size_z + z) * size_x
            boxes[y, z] = lifted_rows[at : at + size_x]
            ends(base[y, z].astype(F32))

    def grouped(boxes, y, z, rows):
        pieces = []
        for u in range(2):
            for v in range(2):
                for w in range(2):
                    pieces.append(boxes[2 * y + v, 2 * z + w][u * rows : (u + 1) * rows])
        return jnp.concatenate(pieces, axis=1)

    coarse, groups = {}, []
    for y in range(size_y // 2):
        for z in range(size_z // 2):
            group = grouped(boxes, y, z, half)
            ends(group)
            middle[y, z] = group.astype(BF)
            groups.append(group.astype(BF))
    lifted_rows = lift(jnp.concatenate(groups, axis=0))
    for y in range(size_y // 2):
        for z in range(size_z // 2):
            at = (y * (size_z // 2) + z) * half
            coarse[y, z] = lifted_rows[at : at + half]
    for y in range(size_y // 4):
        for z in range(size_z // 4):
            group = grouped(coarse, y, z, part)
            ends(group)
            top[y, z] = jnp.concatenate([group, jnp.zeros_like(group)], axis=0).astype(BF)
    fill = [jnp.zeros((-len(lows) % 16, width), F32)]
    low[...] = jnp.concatenate(lows + fill, axis=0).astype(BF)
    high[...] = jnp.concatenate(highs + fill, axis=0).astype(BF)


def lifted(base, weights):
    size_y, size_z, size_x, width = base.shape
    count = size_y * size_z + (size_y // 2) * (size_z // 2) + (size_y // 4) * (size_z // 4)
    ends = jax.ShapeDtypeStruct((-(-count // 16) * 16, width), BF)
    return pl.pallas_call(
        lift_kernel,
        out_shape=(
            jax.ShapeDtypeStruct((size_y // 2, size_z // 2, size_x // 2, width), BF),
            jax.ShapeDtypeStruct((size_y // 4, size_z // 4, size_x // 2, width), BF),
            ends,
            ends,
        ),
        in_specs=[WHOLE] * 2,
        out_specs=(WHOLE,) * 4,
        compiler_params=params(24),
        name="lift",
    )(base, weights)


def turn_operators(weight, blocks, source, at):
    coeffs, _, count = weight.shape
    lanes = blocks.shape[1]
    part = widened(weight[source, :, at : min(at + lanes, count)].astype(F32))
    blocks[pl.ds(at * coeffs + source, lanes, stride=coeffs), :] = widened(part.T)


def number_of(first, second, third):
    number = 0
    for i in range(first * 49 + second * 7 + third):
        number += not all(2 <= j <= 4 for j in (i // 49, i // 7 % 7, i % 7))
    return number


def fill_entry(blocks, table, first, second, third, coeffs):
    def found(at):
        spot = (first, second, at)
        if all(2 <= i <= 4 for i in spot):
            return jnp.zeros((coeffs, blocks.shape[1]), F32)
        before = number_of(*spot)
        return blocks[before * coeffs : (before + 1) * coeffs]

    rows = []
    for s in range(2):
        at = 2 * third + s
        rows.append(found(at + 1) + pltpu.roll(found(at), coeffs, 1))
    rows = jnp.concatenate(rows, axis=0)
    table[third, first, second] = rows[:, : 2 * coeffs].astype(BF)


SLOTS = 8
SHIFTS = [
    (dx, dy, dz)
    for dx in range(3)
    for dy in (1, 0, 2)
    for dz in (1, 0, 2)
    if (dx, dy, dz) != (1, 1, 1)
]


def moved_rows(rows, low, high):
    part = 8
    q = [rows[i : i + part] for i in range(0, rows.shape[0], part)]
    count = len(q)
    before = jnp.concatenate([low, q[-1][:-1]], axis=0)
    after = jnp.concatenate([q[0][1:], high], axis=0)
    if count == 4:
        return [before, q[2], q[0], q[1]], [q[2], q[3], q[1], after]
    if count == 2:
        return [before, q[0]], [q[1], after]
    return [before], [after]


def widened(rows):
    fill = -rows.shape[1] % 128
    if fill:
        zeros = jnp.zeros((rows.shape[0], fill), rows.dtype)
        rows = jnp.concatenate([rows, zeros], axis=1)
    return rows


def store_moved(rows, low, high, copies, y, z, fill=False, wanted=range(3)):
    rows = widened(rows.astype(F32))
    one, two = moved_rows(rows, widened(low), widened(high))
    three = [one, [rows], two]
    for dx in wanted:
        if fill:
            three[dx] = three[dx] + [jnp.zeros_like(rows)]
        copies[dx, y, z] = jnp.concatenate(three[dx], axis=0).astype(BF)


def operator(table, shift, kernels, slot):
    dx, dy, dz = shift
    slot = slot % kernels.shape[0]
    pair = table.shape[4]
    for sx in range(2):
        for sy in range(2):
            parts = [
                table[dz, 2 * dx + sx - tx + 1, 2 * dy + sy - ty + 1]
                for tx in range(2)
                for ty in range(2)
            ]
            at = (2 * sx + sy) * pair
            kernels[slot, at : at + pair] = widened(jnp.concatenate(parts, axis=1))
    rows = kernels.shape[1]
    if rows > 4 * pair:
        kernels[slot, 4 * pair :] = jnp.zeros((rows - 4 * pair, kernels.shape[2]), BF)
    return kernels[slot]


def first_kernel(weight, leaf, below, above, _, table, total, blocks, leaves, kernels):
    coeffs, _, offsets = weight.shape
    size_y, size_z, size_x, width = leaf.shape
    lanes = blocks.shape[1]

    low = below[: size_y * size_z].astype(F32)
    high = above[: size_y * size_z].astype(F32)

    def move(dx):
        steps = []
        for y in range(size_y):
            for z in range(size_z):
                ends = [rows[y * size_z + z : y * size_z + z + 1] for rows in (low, high)]
                steps.append(
                    functools.partial(
                        store_moved, leaf[y, z], *ends, leaves, y, z, wanted=(dx,)
                    )
                )
        return steps

    for step in move(0):
        step()

    def turn(source, carry):
        turn_operators(weight, blocks, source, 0)
        return carry

    lax.fori_loop(0, coeffs, turn, 0, unroll=28)

    tasks = []

    def due(steps, begin, end):
        for i, step in enumerate(steps):
            tasks.append((begin + i * (end - begin) // len(steps), step))

    def needs(shift):
        dx, dy, dz = shift
        return number_of(2 * dx + 2, 2 * dy + 2, 2 * dz + 2)

    begin = 0
    for at in range(lanes, offsets, lanes):
        end = min(slot for slot, shift in enumerate(SHIFTS) if needs(shift) >= at)
        begin = min(begin, end - 1)
        steps = [
            functools.partial(turn_operators, weight, blocks, source, at)
            for source in range(coeffs)
        ]
        due(steps, begin, end)
        begin = end
    for dx in range(1, 3):
        end = min(slot for slot, shift in enumerate(SHIFTS) if shift[0] == dx)
        due(move(dx), end - 8, end)

    done = set()

    def prepare(dx, dy, dz):
        for first in range(2 * dx, 2 * dx + 3):
            for second in range(2 * dy, 2 * dy + 3):
                if (dz, first, second) not in done:
                    done.add((dz, first, second))
                    fill_entry(blocks, table, first, second, dz, coeffs)

    for slot, (dx, dy, dz) in enumerate(SHIFTS):
        prepare(dx, dy, dz)
        kernel = operator(table, (dx, dy, dz), kernels, slot)
        first_z, last_z = max(0, 1 - dz), size_z - max(0, dz - 1)
        first_y, last_y = max(0, 1 - dy), size_y - max(0, dy - 1)
        count = (last_z - first_z) * size_x
        rows = leaves[
            dx, first_y + dy - 1 : last_y + dy - 1, first_z + dz - 1 : last_z + dz - 1
        ].reshape(-1, leaves.shape[4])
        product = jnp.dot(rows, kernel, preferred_element_type=F32)
        for i in range(last_y - first_y):
            at = ((first_y + i) * size_z + first_z) * size_x
            piece = product[i * count : (i + 1) * count]
            total[at : at + count] = piece if slot == 0 else total[at : at + count] + piece
        for when, step in tasks:
            if when == slot:
                step()
    for dx, dy, dz in [(dx, dy, dz) for dx in range(3) for dy in range(3) for dz in range(3)]:
        prepare(dx, dy, dz)


def first_part(transfer_weight, leaf, below, above, after):
    count, coeffs, _ = transfer_weight.shape
    size_y, size_z, size_x, width = leaf.shape
    wide = -(-width // 128) * 128
    return pl.pallas_call(
        first_kernel,
        out_shape=(
            jax.ShapeDtypeStruct((3, 7, 7, 2 * coeffs, 2 * coeffs), BF),
            jax.ShapeDtypeStruct((size_y * size_z * size_x, wide), F32),
        ),
        in_specs=[WHOLE] * 4 + [ANYWHERE],
        out_specs=(WHOLE, WHOLE),
        scratch_shapes=[
            pltpu.VMEM((-(-count // 128) * 128 * coeffs, 128), F32),
            pltpu.VMEM((3, size_y, size_z, size_x, wide), BF),
            pltpu.VMEM((SLOTS, wide, wide), BF),
        ],
        compiler_params=params(32),
        cost_estimate=pl.CostEstimate(flops=2 * 10**10, bytes_accessed=10**7, transcendentals=0),
        name="first",
    )(transfer_weight.transpose(1, 2, 0), leaf, below, above, after)


def far_kernel(
    odd, near, table, middle, top, below_x, above_x, got_z, got_y, got_yz, down, out,
    total, leaves, middles, tops, kernels, upper, out_rows, sent,
):
    size_y, size_z = 2 * middle.shape[0], 2 * middle.shape[1]
    half, width = middle.shape[2:]
    size_x = 2 * half
    coeffs = width // 8
    none = jnp.zeros((1, width), F32)
    odd_y, odd_z = odd[0] == 1, odd[1] == 1

    def chosen(is_odd, side, got, rows):
        first, other = got[0, rows], got[1, rows]
        pair = (first, other) if side == 0 else (other, first)
        return jnp.where(is_odd, pair[0], pair[1])

    def corner(side_y, side_z, rows):
        near_y = [chosen(odd_z, side_z, got_yz.at[i], rows) for i in range(2)]
        pair = near_y if side_y == 0 else near_y[::-1]
        return jnp.where(odd_y, pair[0], pair[1])

    sizes = [(size_y, size_z, size_x), (size_y // 2, size_z // 2, half), (size_y // 4, size_z // 4, half)]
    own = (None, middle, top)
    slabs = [{}, {}, {}]
    at_x = 0
    sides_x = [below_x[...].astype(F32), above_x[...].astype(F32)]
    for level, (count_y, count_z, rows) in enumerate(sizes):
        for y in range(count_y):
            for z in range(count_z):
                if level > 0:
                    ends = [side[at_x : at_x + 1] for side in sides_x]
                    slabs[level][y + 1, z + 1] = [own[level][y, z], *ends]
                at_x += 1

    def unpack(read, spots):
        at = 0
        for level, (_, _, rows) in enumerate(sizes):
            for spot in spots(level):
                slabs[level][spot] = [read(slice(at, at + rows))]
                at += rows
        count = 2 * sum(len(spots(level)) for level in range(3))
        tail = read(slice(at, at + -(-count // 16) * 16)).astype(F32)
        at = 0
        for level in range(3):
            for end in range(2):
                for spot in spots(level):
                    slabs[level][spot].append(tail[at : at + 1])
                    at += 1

    for side in range(2):
        unpack(
            functools.partial(chosen, odd_z, side, got_z),
            lambda level: [(y + 1, side * (sizes[level][1] + 1)) for y in range(sizes[level][0])],
        )
        unpack(
            functools.partial(chosen, odd_y, side, got_y),
            lambda level: [(side * (sizes[level][0] + 1), z + 1) for z in range(sizes[level][1])],
        )
        for other in range(2):
            unpack(
                functools.partial(corner, side, other),
                lambda level: [(side * (sizes[level][0] + 1), other * (sizes[level][1] + 1))],
            )

    copies = (leaves, middles, tops)

    def move(level, wanted):
        steps = []
        for (y, z), (rows, low, high) in slabs[level].items():
            if level == 2:
                rows = rows[: half // 2]
            steps.append(
                functools.partial(
                    store_moved, rows, low, high, copies[level], y, z, level == 2, wanted
                )
            )
        return steps

    for step in move(1, (0,)) + move(2, (0,)):
        step()
    tasks = []

    def due(steps, begin, end):
        for i, step in enumerate(steps):
            tasks.append((begin + i * (end - begin) // len(steps), step))

    for dx in range(1, 3):
        end = min(slot for slot, shift in enumerate(SHIFTS) if shift[0] == dx)
        due(move(1, (dx,)) + move(2, (dx,)), end - 8, end)
    due(move(0, range(3)), 0, len(SHIFTS))

    leaf_rows = size_y * size_z * size_x
    wide = kernels.shape[1]
    made = []
    for slot, (dx, dy, dz) in enumerate(SHIFTS):
        made.append(operator(table, (dx, dy, dz), kernels, slot))
        rows = [
            middles[dx, dy : dy + size_y // 2, dz : dz + size_z // 2].reshape(-1, wide),
            tops[dx, dy : dy + size_y // 4, dz : dz + size_z // 4].reshape(-1, wide),
        ]
        rows = jnp.concatenate(rows, axis=0)
        product = jnp.dot(rows, made[slot], preferred_element_type=F32)[:, :width]
        upper[...] = product if slot == 0 else upper[...] + product
        for when, step in tasks:
            if when == slot:
                step()

    weight = down[down.shape[0] // 2 :][:coeffs]

    def spread(count_y, count_z, parent, rows):
        pieces = []
        for y in range(2 * count_y):
            for z in range(2 * count_z):
                for u in range(2):
                    octant = 4 * u + 2 * (y % 2) + z % 2
                    values = parent(y // 2, z // 2)
                    pieces.append(values[:rows, octant * coeffs : (octant + 1) * coeffs])
        return jnp.concatenate(pieces, axis=0).astype(BF)

    middle_rows = leaf_rows // 8

    def top_of(y, z):
        at = middle_rows + (y * (size_z // 4) + z) * half
        return upper[at : at + half]

    boxes = spread(size_y // 4, size_z // 4, top_of, half // 2)
    local = upper[:middle_rows] + jnp.dot(boxes, weight, preferred_element_type=F32)

    def middle_of(y, z):
        at = (y * (size_z // 2) + z) * half
        return local[at : at + half]

    boxes = spread(size_y // 2, size_z // 2, middle_of, half)
    part_x = half // 2
    step = size_z * size_x
    touched = set()

    def finish(y):
        part = slice(y * step, (y + 1) * step)
        product = []

        def add(z):
            if not product:
                product.append(jnp.dot(boxes[part], weight, preferred_element_type=F32))
            at = z * size_x
            here = slice(y * step + at, y * step + at + size_x)
            source = total if here.start in touched else near
            rows = source[here] + widened(product[0][at : at + size_x])
            for i in range(size_x):
                a, b, x = i // half, i // part_x % 2, i % part_x
                out_rows[4 * x + 2 * b + a, y, z : z + 1] = rows[i : i + 1, :width]

        return [functools.partial(add, z) for z in range(size_z)]

    leaving = []

    def leave(ys):
        rows = pl.ds(ys.start, len(ys))
        copy = pltpu.make_async_copy(out_rows.at[:, rows], out.at[:, rows], sent.at[len(leaving)])
        copy.start()
        leaving.append(copy)

    steps = []
    halves = [range(0, size_y // 2), range(size_y // 2, size_y)]
    for ys in halves:
        count = -(-len(steps) // (len(SHIFTS) - 2))
        for slot, (dx, dy, dz) in enumerate(SHIFTS):
            places, rows = [], []
            for y in ys:
                for z in range(size_z):
                    if y + dy in (0, size_y + 1) or z + dz in (0, size_z + 1):
                        places.append((y * size_z + z) * size_x)
                        rows.append(leaves[dx, y + dy, z + dz])
            if rows:
                rows = jnp.concatenate(rows, axis=0)
                product = jnp.dot(rows, kernels[slot], preferred_element_type=F32)
                for i, at in enumerate(places):
                    source = total if at in touched else near
                    touched.add(at)
                    total[at : at + size_x] = (
                        source[at : at + size_x] + product[i * size_x : (i + 1) * size_x]
                    )
            for one in steps[:count]:
                one()
            steps = steps[count:]
        assert not steps
        if ys is not halves[0]:
            leave(halves[0])
        steps = [one for y in ys for one in finish(y)]
    for one in steps:
        one()
    leave(halves[1])
    for copy in leaving:
        copy.wait()


def far(odd, near, table, middle, top, halos, down):
    rows, wide = near.shape
    width = middle.shape[3]
    size_y, size_z, half = 2 * middle.shape[0], 2 * middle.shape[1], middle.shape[2]
    upper = half * ((size_y // 2) * (size_z // 2) + (size_y // 4) * (size_z // 4))
    return pl.pallas_call(
        far_kernel,
        out_shape=jax.ShapeDtypeStruct((2 * half, size_y, size_z, width), F32),
        in_specs=[pl.BlockSpec(memory_space=pltpu.SMEM)] + [WHOLE] * 10,
        out_specs=HBM,
        scratch_shapes=[
            pltpu.VMEM((rows, wide), F32),
            pltpu.VMEM((3, size_y + 2, size_z + 2, 2 * half, wide), BF),
            pltpu.VMEM((3, size_y // 2 + 2, size_z // 2 + 2, half, wide), BF),
            pltpu.VMEM((3, size_y // 4 + 2, size_z // 4 + 2, half, wide), BF),
            pltpu.VMEM((len(SHIFTS), wide, wide), BF),
            pltpu.VMEM((upper, width), F32),
            pltpu.VMEM((2 * half, size_y, size_z, width), F32),
            pltpu.SemaphoreType.DMA((2,)),
        ],
        compiler_params=params(42),
        name="far",
    )(odd, near, table, middle, top, *halos, down)


def shards(densities, upward_weight, transfer_weight, downward_weight):
    size_x, size_y, size_z, width = densities.shape
    fill = ((0, -downward_weight.shape[0] % 16), (0, 0))
    weights = [jnp.pad(upward_weight.T, fill), jnp.pad(downward_weight, fill)]
    weights = jnp.concatenate(weights, axis=0)
    base = densities.reshape(size_x // 4, 2, 2, size_y, size_z, width)
    base = base.transpose(3, 4, 2, 1, 0, 5).reshape(size_y, size_z, size_x, width)
    middle, top, low, high = lifted(base, weights)
    levels = [base, middle, top]

    def packed(pieces):
        rows = jnp.concatenate([piece.reshape(-1, width) for piece in pieces], axis=0)
        return jnp.pad(rows, ((0, -rows.shape[0] % 16), (0, 0)))

    def unpacked(flat, shapes):
        pieces, at = [], 0
        for shape in shapes:
            count = 1
            for extent in shape:
                count *= extent
            pieces.append(flat[at : at + count].reshape(shape + (width,)))
            at += count
        return pieces

    first, other = exchange(low, high, "gx")
    odd = is_odd("gx")
    below_x, above_x = jnp.where(odd, first, other), jnp.where(odd, other, first)
    shapes = [level.shape[:2] for level in levels]
    sides = [
        jnp.stack(both) for both in zip(unpacked(below_x, shapes), unpacked(above_x, shapes))
    ]

    def face_z(at):
        return packed([level[:, at] for level in levels] + [side[:, :, at] for side in sides])

    def face_y(at):
        return packed([level[at] for level in levels] + [side[:, at] for side in sides])

    def corner(at_y, at_z):
        rows = [level[at_y, at_z] for level in levels] + [side[:, at_y, at_z] for side in sides]
        return packed(rows)

    low_z = face_z(0)
    got_z = jnp.stack(exchange(low_z, face_z(-1), "gz"))
    got_y = jnp.stack(exchange(face_y(0), face_y(-1), "gy"))
    got_yz = exchange_corners([[corner(y, z) for z in (0, -1)] for y in (0, -1)], "gy", "gz")
    table, near = first_part(transfer_weight, base, below_x, above_x, low_z)
    odd = jnp.stack([is_odd("gy"), is_odd("gz")]).astype(jnp.int32)
    halos = (below_x, above_x, got_z, got_y, got_yz)
    return far(odd, near, table, middle, top, halos, weights)


def solution(mesh):
    placed = (P("gx", "gy", "gz", None), P(), P(), P())
    return jax.shard_map(
        shards, mesh=mesh, in_specs=placed, out_specs=P("gx", "gy", "gz", None), check_vma=False
    )
```
